256 devices in a mesh: section: 8 (over x, core), vocab: 32 (over y, z).
Axes of the slice: x: 4, y: 4, z: 8, core: 2. Of those that a mesh axis runs over, the one named last changes fastest.
Arguments:
- hidden: bfloat16 [2048, 8192], P('section', 'vocab'), may hold values from -1000 to 1000
- norm_gain: float32 [8192], P('vocab'), may hold values from 0.5 to 1.5
- head_weight: bfloat16 [8192, 98304], P(None, ('section', 'vocab')), may hold values from -5 to 5
- exit_mask: int32 [2048], replicated, may hold values from 0 to 1, as said below
- targets: int32 [2048], replicated, may hold values from 0 to 98303
- section_weight: float32 [8], replicated, may hold values from 8 to 24
Outputs:
- mean_loss: float32 [], replicated
- d_hidden: bfloat16 [2048, 8192], P('section', 'vocab')
- d_gain: float32 [8192], P('vocab')
- d_head: bfloat16 [8192, 98304], P(None, ('section', 'vocab'))
The draws below stay inside these ranges and needn't reach their ends.
Inputs may be any that keep to these rules, and one draw needn't show every extreme that they name: `exit_mask`: exactly 384 ones in all; at most 96 ones among the 256 tokens of one section group, and exactly 96 in some section group.
All inputs are finite; a program needn't handle non-finite values.
Results may differ from the reference program's by a relative error of at most 0.027.
Values may be sent and summed in bfloat16 or wider, within the bound.
No kernel may reach another device: no remote copies, remote signals or barrier semaphores. Data moves between devices by JAX's collectives and lax.ppermute only.
A program may use at most 128 MiB of HBM per device.

```python
import math
import jax
import jax.numpy as jnp
import numpy as np
from jax import lax

D = 8192
VOCAB_DEV = 384
TOK = 256
CAP = 96
EXIT_MEAN = 48
SECTIONS = 8
VOCAB = 98304
EXITS = 384
N_SECTION = 8
N_VOCAB = 32


def shuffle_tokens(one_key):
    return jax.random.permutation(one_key, TOK)


def exit_pattern(key):
    key = jax.random.fold_in(key, 101)
    key_delta, key_order, key_rank = jax.random.split(key, 3)
    others_count = SECTIONS - 1
    spare = EXIT_MEAN * SECTIONS - CAP
    base_count = spare // others_count
    remainder = spare % others_count
    spread = base_count // 2
    others = base_count + (jnp.arange(others_count) < remainder).astype(jnp.int32)
    pairs = others_count // 2
    shifts = jax.random.randint(key_delta, (pairs,), -spread, spread + 1).astype(jnp.int32)
    delta = jnp.concatenate([shifts, -shifts, jnp.zeros((others_count - 2 * pairs,), jnp.int32)])
    counts = jnp.concatenate([jnp.full((1,), CAP, jnp.int32), (others + delta).astype(jnp.int32)])
    counts = jax.random.permutation(key_order, counts)
    ranks = jax.vmap(shuffle_tokens)(jax.random.split(key_rank, SECTIONS))
    return (ranks.astype(jnp.int32), counts)


def draw_hidden(key, part):
    key = jax.random.fold_in(key, 3)
    key_body, key_row, key_col = jax.random.split(key, 3)
    col_scale = jnp.exp(jnp.linspace(0.0, math.log(3.0), D)) * jnp.exp(jax.random.uniform(key_col, (D,), minval=0.0, maxval=math.log(3.3)))
    row_scale = jnp.exp(jax.random.uniform(key_row, (SECTIONS * TOK, 1), minval=0.0, maxval=math.log(10.0)))
    values = jax.random.normal(key_body, (SECTIONS * TOK, D)) * row_scale * col_scale[None, :]
    return values.astype(jnp.bfloat16)


def draw_head_weight(key, part):
    key = jax.random.fold_in(key, 5)
    scale = 3.0 / math.sqrt(D)
    values = jax.random.normal(key, (D, VOCAB)) * scale
    return values.astype(jnp.bfloat16)


def draw_exit_mask(key, part):
    ranks, counts = exit_pattern(key)
    return (ranks < counts[:, None]).astype(jnp.int32).reshape(-1)


def with_ends(array, key, smallest, largest):
    longest = array.shape.index(max(array.shape))
    spots = []
    for shift in (0, 1):
        where = [jax.random.randint(jax.random.fold_in(key, axis), (), 0, length) for axis, length in enumerate(array.shape)]
        where[longest] = (where[longest] + shift) % array.shape[longest]
        spots.append(tuple(where))
    return array.at[spots[0]].set(smallest).at[spots[1]].set(largest)


def skewed_wide(own_key, shape, amount, skew):
    portions = [min(1 << octave, amount + 1 - (1 << octave)) * (1 << 20) // math.isqrt((1 << octave) ** skew) + 1 for octave in range((amount + 1).bit_length()) if 1 << octave <= amount]
    deviation = 1 + sum(portions) // (1 << 30)
    table = np.cumsum(np.array([max(1, weight // deviation) for weight in portions]))
    ticket = jax.random.randint(jax.random.fold_in(own_key, 1), shape, 0, int(table[len(portions) - 1]))
    start = jnp.left_shift(1, jnp.searchsorted(jnp.asarray(table, jnp.int32), ticket, side="right").astype(jnp.int32))
    grade = start - 1 + jax.random.randint(jax.random.fold_in(own_key, 4), shape, 0, 1 << 30) % jnp.minimum(start, amount + 1 - start)
    return jax.random.permutation(jax.random.fold_in(own_key, 2), amount)[grade].astype(jnp.int32)


def setup_inputs(seed: int = 0) -> dict:
    splits = jax.random.split(jax.random.key(seed), 7)
    hidden = draw_hidden(jax.random.fold_in(splits[6], 71), 0)
    norm_gain = jnp.clip(1.0 + 0.1 * jax.random.normal(splits[1], (D,), jnp.float32), 0.5, 1.5)
    head_weight = draw_head_weight(jax.random.fold_in(splits[6], 71), 0)
    exit_mask = draw_exit_mask(jax.random.fold_in(splits[6], 71), 0)
    targets = with_ends(skewed_wide(splits[4], (SECTIONS * TOK,), VOCAB, 1), jax.random.fold_in(splits[4], 3), 0, VOCAB - 1).astype(jnp.int32)
    section_weight = jnp.clip(jnp.exp(jax.random.uniform(splits[5], (SECTIONS,), jnp.float32, math.log(8.0), math.log(24.0))), 8.0, 24.0)
    return dict(hidden=hidden, norm_gain=norm_gain, head_weight=head_weight, exit_mask=exit_mask, targets=targets, section_weight=section_weight)


epsilon = 1e-05

def reference(hidden, norm_gain, head_weight, exit_mask, targets, section_weight):
    indices = jnp.nonzero(exit_mask, size=EXITS)[0].astype(jnp.int32)
    exit_rows = hidden[indices].astype(jnp.float32)
    inverse = lax.rsqrt(lax.optimization_barrier(jnp.mean(exit_rows * exit_rows, axis=1)) + epsilon)
    normed = (exit_rows * inverse[:, None] * norm_gain[None, :]).astype(jnp.bfloat16)
    logits = jnp.dot(normed, head_weight, preferred_element_type=jnp.float32)
    row_peak = lax.optimization_barrier(jnp.max(logits, axis=1))
    row_total = lax.optimization_barrier(jnp.sum(jnp.exp(logits - row_peak[:, None]), axis=1))
    logsum = row_peak + jnp.log(row_total)
    labels = targets[indices]
    onehot = (jnp.arange(VOCAB, dtype=jnp.int32)[None, :] == labels[:, None]).astype(jnp.float32)
    picked = lax.optimization_barrier(jnp.sum(logits * onehot, axis=1))
    mean_loss = jnp.sum(logsum - picked) / EXITS
    weights = section_weight[indices // TOK]
    softmax_rows = jnp.exp(logits - logsum[:, None])
    dlogits = (weights[:, None] * (softmax_rows - onehot)).astype(jnp.bfloat16)
    d_head = jnp.dot(normed.T, dlogits, preferred_element_type=jnp.float32).astype(jnp.bfloat16)
    block_count = N_SECTION * N_VOCAB
    dlogit_blocks = jnp.transpose(dlogits.reshape(EXITS, block_count, VOCAB_DEV), (1, 0, 2))
    head_blocks = jnp.transpose(head_weight.reshape(D, block_count, VOCAB_DEV), (1, 0, 2))

    def add_block(total, pair):
        block_grad, block_head = pair
        partial_value = lax.dot_general(block_grad, block_head, (((1,), (1,)), ((), ())), preferred_element_type=jnp.float32).astype(jnp.bfloat16)
        return (total + partial_value.astype(jnp.float32), None)
    d_normed, _ = lax.scan(add_block, jnp.zeros((EXITS, D), jnp.float32), (dlogit_blocks, head_blocks))
    scaled = d_normed * norm_gain[None, :]
    inner_dots = lax.optimization_barrier(jnp.mean(scaled * exit_rows, axis=1))
    d_rows = inverse[:, None] * scaled - exit_rows * (inverse * inverse * inverse * inner_dots)[:, None]
    d_gain = lax.optimization_barrier(jnp.sum(d_normed * exit_rows * inverse[:, None], axis=0))
    d_hidden = jnp.zeros(hidden.shape, jnp.float32).at[indices].set(d_rows).astype(jnp.bfloat16)
    return (mean_loss, d_hidden, d_gain, d_head)
```

```python
import functools

import jax
import jax.numpy as jnp
import numpy as np
from jax import lax
from jax.experimental import pallas as pl
from jax.experimental.pallas import tpu as pltpu
from jax.sharding import Mesh, PartitionSpec as P

D = 8192
CAP = 96
EXITS = 384
NX, NC, NY, NZ = 4, 2, 4, 8
NV = NY * NZ
NA, NB = 4, 8
AXES = ("x", "core", "y", "z")
HALF = 128
VDEV = 384
ROWS = EXITS + 16

epsilon = 1e-05
f32 = jnp.float32
bf16 = jnp.bfloat16
VMEM_BYTES = 48 * 1024 * 1024


def spot(core, y, z):
    if core == 0:
        return y, z
    return z // 2, (y if z % 2 == 0 else 7 - y)


def device(core, a, b):
    if core == 0:
        return a, b
    return (b, 2 * a) if b < 4 else (7 - b, 2 * a + 1)


def pairs(da, db):
    out = []
    for core in range(NC):
        for y in range(NY):
            for z in range(NZ):
                a, b = spot(core, y, z)
                ty, tz = device(core, (a + da) % NA, (b + db) % NB)
                out.append(((core * NY + y) * NZ + z, (core * NY + ty) * NZ + tz))
    return out


TABLE = np.zeros((NC, NY, NZ, NV), np.int32)
for _core in range(NC):
    for _y in range(NY):
        for _z in range(NZ):
            _a, _b = spot(_core, _y, _z)
            for _r in range(NV):
                _ty, _tz = device(_core, (_a + _r % NA) % NA, (_b + _r // NA) % NB)
                TABLE[_core, _y, _z, _r] = _ty * NZ + _tz


def send_a(value, step):
    return lax.ppermute(value, ("core", "y", "z"), pairs(step, 0))


def send_b(value, step):
    return lax.ppermute(value, ("core", "y", "z"), pairs(0, step))


def shift(value, axis, step):
    n = {"x": NX, "y": NY, "z": NZ}[axis]
    return lax.ppermute(value, axis, [(i, (i + step) % n) for i in range(n)])


def swap(value):
    return lax.ppermute(value, "core", [(0, 1), (1, 0)])


def tree(parts):
    parts = list(parts)
    while len(parts) > 1:
        h = len(parts) // 2
        parts = [parts[i] + parts[i + h] for i in range(h)]
    return parts[0]


def merge(stats, axis):
    if axis != "z":
        parts = [stats, shift(stats, axis, -1), shift(stats, axis, 2), shift(stats, axis, 1)]
    else:
        down, up = shift(stats, axis, -1), shift(stats, axis, 1)
        near = jnp.concatenate([up, stats, down], axis=0)
        high, low = shift(near, axis, -3), shift(near[8:], axis, 3)
        high, low = high.reshape(3, 8, -1), low.reshape(2, 8, -1)
        parts = [stats, down, high[0], high[1], high[2], low[0], low[1], up]
    peak = parts[0][0]
    for p in parts[1:]:
        peak = jnp.maximum(peak, p[0])
    rows = []
    for p in parts:
        gap = p[0] - peak
        scale = jnp.exp(gap)
        rows.append(jnp.stack([p[1] * scale, scale * (p[2] + p[1] * gap), p[3]]))
    return jnp.concatenate([peak[None], tree(rows), stats[4:]], axis=0)


def weight_specs(places):
    own = [
        pl.BlockSpec((HALF, VDEV), lambda i, t, r=r: (t[r] * 2 + t[NV], 0)) for r in places
    ]
    got = [pl.BlockSpec((HALF, VDEV), lambda i, t, r=r: (t[r], 0)) for r in places]
    return own + got


def whole(shape):
    return pl.BlockSpec(shape, lambda i, t: (0,) * len(shape))


def params():
    return pltpu.CompilerParams(
        vmem_limit_bytes=VMEM_BYTES, dimension_semantics=("arbitrary",)
    )


def cost(flops, moved):
    return pl.CostEstimate(flops=flops, bytes_accessed=moved, transcendentals=0)


def add_logits(table, head_weight, other, blocks, places, before):
    n, m = len(places), len(blocks)

    def kernel(t, *refs):
        own, got = refs[:n], refs[n : 2 * n]
        acts, rest = refs[2 * n : 2 * n + m], refs[2 * n + m :]
        out = rest[-1]
        pieces = [ref[k] for ref in acts for k in range(ref.shape[0])]
        left = jnp.concatenate([p[:EXITS] for p in pieces], axis=1)
        squares = sum(p[EXITS:].astype(f32) for p in pieces)
        tail = jnp.concatenate([squares, jnp.zeros((16, 2 * VDEV - HALF), f32)], axis=1)
        for side, ws in ((0, own), (VDEV, got)):
            w = jnp.concatenate([ref[...] for ref in ws], axis=0)
            value = jnp.dot(left, w, preferred_element_type=f32)
            if before is not None:
                value += rest[0][:EXITS, side : side + VDEV]
            out[:EXITS, side : side + VDEV] = value
        if before is not None:
            tail += rest[0][EXITS:, :]
        out[EXITS:, :] = tail

    more = [] if before is None else [before]
    return pl.pallas_call(
        kernel,
        out_shape=jax.ShapeDtypeStruct((ROWS, 2 * VDEV), f32),
        grid_spec=pltpu.PrefetchScalarGridSpec(
            num_scalar_prefetch=1,
            grid=(1,),
            in_specs=weight_specs(places)
            + [whole(b.shape) for b in blocks]
            + [whole((ROWS, 2 * VDEV)) for _ in more],
            out_specs=whole((ROWS, 2 * VDEV)),
        ),
        compiler_params=params(),
        cost_estimate=cost(2 * EXITS * HALF * n * 2 * VDEV, 300_000 * n + 2_400_000),
        name="add_logits",
    )(table, *[head_weight] * n, *[other] * n, *blocks, *more)


def gradient_blocks(table, head_weight, other, dl_own, dl_got, places, sizes):
    n = len(places)

    def kernel(t, *refs):
        own, got = refs[:n], refs[n : 2 * n]
        a, b = refs[2 * n][...], refs[2 * n + 1][...]
        outs = refs[2 * n + 2 :]
        spots = [(ref, k) for ref in outs for k in range(ref.shape[0])]
        contract = (((1,), (1,)), ((), ()))
        for k in range(0, n, 2):
            w = jnp.concatenate([own[k][...], own[k + 1][...]], axis=0)
            v = jnp.concatenate([got[k][...], got[k + 1][...]], axis=0)
            value = lax.dot_general(a, w, contract, preferred_element_type=f32)
            value += lax.dot_general(b, v, contract, preferred_element_type=f32)
            for j in range(2):
                ref, q = spots[k + j]
                ref[q] = value[:, j * HALF : (j + 1) * HALF].astype(bf16)

    return pl.pallas_call(
        kernel,
        out_shape=tuple(jax.ShapeDtypeStruct((s, EXITS, HALF), bf16) for s in sizes),
        grid_spec=pltpu.PrefetchScalarGridSpec(
            num_scalar_prefetch=1,
            grid=(1,),
            in_specs=weight_specs(places) + [whole((EXITS, VDEV))] * 2,
            out_specs=tuple(whole((s, EXITS, HALF)) for s in sizes),
        ),
        compiler_params=params(),
        cost_estimate=cost(2 * EXITS * HALF * n * 2 * VDEV, 300_000 * n + 600_000),
        name="gradient_blocks",
    )(table, *[head_weight] * n, *[other] * n, dl_own, dl_got)


def eye():
    shape = (HALF, HALF)
    return lax.broadcasted_iota(jnp.int32, shape, 0) == lax.broadcasted_iota(jnp.int32, shape, 1)


def to_column(row):
    same = eye()
    return jnp.concatenate(
        [
            jnp.sum(jnp.where(same, row[:, k : k + HALF], 0.0), axis=1, keepdims=True)
            for k in range(0, EXITS, HALF)
        ],
        axis=0,
    )


def to_row(column):
    same = eye()
    return jnp.concatenate(
        [
            jnp.sum(jnp.where(same, column[k : k + HALF], 0.0), axis=0, keepdims=True)
            for k in range(0, EXITS, HALF)
        ],
        axis=1,
    )


def softmax_parts(starts, labels, part, got):
    def kernel(starts, lab, part, got, logits, stats):
        sq = part[EXITS:, :HALF] + got[EXITS:, :HALF]
        sq = sq[0:3] + sq[3:6] + sq[6:9]
        sq = jnp.concatenate([sq[0:1], sq[1:2], sq[2:3]], axis=1)
        inverse = lax.rsqrt(to_column(sq) / D + epsilon)
        sides = []
        for side in range(2):
            a, b = side * VDEV, (1 - side) * VDEV
            value = (part[:EXITS, a : a + VDEV] + got[:EXITS, b : b + VDEV]) * inverse
            logits[:, a : a + VDEV] = value
            sides.append(value)
        peak = jnp.maximum(
            jnp.max(sides[0], axis=1, keepdims=True), jnp.max(sides[1], axis=1, keepdims=True)
        )
        sums = []
        for side, value in enumerate(sides):
            gap = value - peak
            power = jnp.exp(gap)
            ids = lax.broadcasted_iota(jnp.int32, (EXITS, VDEV), 1) + starts[side]
            hit = jnp.where(ids == lab[...], value, 0.0)
            sums.append(
                [jnp.sum(q, axis=1, keepdims=True) for q in (power, power * gap, hit)]
            )
        cols = [peak] + [p + q for p, q in zip(*sums, strict=True)] + [inverse]
        rows = [to_row(q) for q in cols] + [jnp.zeros((3, EXITS), f32)]
        stats[...] = jnp.concatenate(rows, axis=0)

    return pl.pallas_call(
        kernel,
        out_shape=(
            jax.ShapeDtypeStruct((EXITS, 2 * VDEV), f32),
            jax.ShapeDtypeStruct((8, EXITS), f32),
        ),
        grid_spec=pltpu.PrefetchScalarGridSpec(
            num_scalar_prefetch=1,
            grid=(1,),
            in_specs=[whole((EXITS, 1)), whole((ROWS, 2 * VDEV)), whole((ROWS, 2 * VDEV))],
            out_specs=(whole((EXITS, 2 * VDEV)), whole((8, EXITS))),
        ),
        compiler_params=params(),
        cost_estimate=cost(3_000_000, 3_700_000),
        name="softmax_parts",
    )(starts, labels, part, got)


def logit_gradients(starts, labels, weight, logits, stats):
    def kernel(starts, lab, w, logits, stats, dl_own, dl_got, scaled):
        logsum = to_column(stats[0:1] + jnp.log(stats[1:2]))
        inverse = to_column(stats[4:5])
        for side, out in ((0, dl_own), (1, dl_got)):
            a = side * VDEV
            soft = jnp.exp(logits[:, a : a + VDEV] - logsum)
            ids = lax.broadcasted_iota(jnp.int32, (EXITS, VDEV), 1) + starts[side]
            value = w[...] * (soft - jnp.where(ids == lab[...], 1.0, 0.0))
            out[...] = value.astype(bf16)
            if side == 0:
                scaled[...] = (value * inverse).astype(bf16)

    return pl.pallas_call(
        kernel,
        out_shape=tuple(jax.ShapeDtypeStruct((EXITS, VDEV), bf16) for _ in range(3)),
        grid_spec=pltpu.PrefetchScalarGridSpec(
            num_scalar_prefetch=1,
            grid=(1,),
            in_specs=[
                whole((EXITS, 1)),
                whole((EXITS, 1)),
                whole((EXITS, 2 * VDEV)),
                whole((8, EXITS)),
            ],
            out_specs=tuple(whole((EXITS, VDEV)) for _ in range(3)),
        ),
        compiler_params=params(),
        cost_estimate=cost(2_000_000, 2_100_000),
        name="logit_gradients",
    )(starts, labels, weight, logits, stats)


def head_gradient(where, own, got, dl):
    per = 2

    def kernel(t, *refs):
        d, out = refs[-2], refs[-1]
        first = t[2 * NV] == 0
        lanes = []
        for k in range(per):
            p, q = refs[k][0], refs[per + k][0]
            lanes += [jnp.where(first, p, q), jnp.where(first, q, p)]
        left = jnp.concatenate(lanes, axis=1)
        out[...] = lax.dot_general(
            left, d[...], (((0,), (0,)), ((), ())), preferred_element_type=f32
        ).astype(bf16)

    def block(base, k):
        return pl.BlockSpec((1, EXITS, HALF), lambda i, t: (t[base + i * per + k], 0, 0))

    return pl.pallas_call(
        kernel,
        out_shape=jax.ShapeDtypeStruct((D, VDEV), bf16),
        grid_spec=pltpu.PrefetchScalarGridSpec(
            num_scalar_prefetch=1,
            grid=(NV // per,),
            in_specs=[block(0, k) for k in range(per)]
            + [block(NV, k) for k in range(per)]
            + [whole((EXITS, VDEV))],
            out_specs=pl.BlockSpec((2 * HALF * per, VDEV), lambda i, t: (i, 0)),
        ),
        compiler_params=params(),
        cost_estimate=cost(2 * EXITS * D * VDEV, 13_000_000),
        name="head_gradient",
    )(where, *[own] * per, *[got] * per, dl)


def body(hidden, norm_gain, head_weight, exit_mask, targets, section_weight):
    x, c = lax.axis_index("x"), lax.axis_index("core")
    y, z = lax.axis_index("y"), lax.axis_index("z")
    section = x * NC + c
    sections = NX * NC
    tokens = hidden.shape[0]

    split = head_weight.reshape(NV, NC, HALF, VDEV)
    other = swap(lax.dynamic_index_in_dim(split, 1 - c, 1, keepdims=False).reshape(D // 2, VDEV))
    tables = jnp.asarray(TABLE)
    spots = lax.dynamic_slice(tables, (0, y, z, 0), (NC, 1, 1, NV)).reshape(NC, NV)
    mine = lax.dynamic_index_in_dim(spots, c, 0, keepdims=False)
    theirs = lax.dynamic_index_in_dim(spots, 1 - c, 0, keepdims=False)
    c_one = c.astype(jnp.int32)[None]
    table = jnp.concatenate([mine, c_one])
    slices = jnp.arange(NV, dtype=jnp.int32)

    def inverse_of(t):
        return jnp.sum(jnp.where(t[None, :] == slices[:, None], slices[None, :], 0), axis=1)

    where = jnp.concatenate([inverse_of(mine), inverse_of(theirs), c_one])

    mask = exit_mask.reshape(sections, tokens)
    rank = jnp.cumsum(mask, axis=1) - 1
    count = jnp.sum(mask, axis=1)
    end = jnp.cumsum(count)
    base = end - count
    slot = jnp.arange(CAP, dtype=jnp.int32)
    own_rank = lax.dynamic_index_in_dim(rank, section, 0, keepdims=False)
    own_mask = lax.dynamic_index_in_dim(mask, section, 0, keepdims=False)
    own_hit = ((own_rank[None, :] == slot[:, None]) & (own_mask[None, :] == 1)).astype(bf16)
    row = jnp.arange(EXITS, dtype=jnp.int32)
    row_section = jnp.sum((row[:, None] >= end[None, :]).astype(jnp.int32), axis=1)
    row_weight = jnp.sum(
        jnp.where(row_section[:, None] == jnp.arange(sections)[None, :], section_weight[None, :], 0.0),
        axis=1,
    )
    place_of = jnp.where(mask == 1, rank + base[:, None], -1).reshape(-1)
    labels = jnp.sum(jnp.where(place_of[None, :] == row[:, None], targets[None, :], 0), axis=1)
    weight_col, label_col = row_weight[:, None], labels[:, None]

    rows_own = jnp.dot(own_hit, hidden, preferred_element_type=f32).astype(bf16)
    halves = rows_own.reshape(CAP, NC, HALF)
    keep = lax.dynamic_index_in_dim(halves, c, 1, keepdims=False)
    came = swap(lax.dynamic_index_in_dim(halves, 1 - c, 1, keepdims=False))
    pair = jnp.concatenate(
        [jnp.where(c == 0, keep, came), jnp.where(c == 0, came, keep)], axis=0
    )
    slots = jnp.concatenate(
        [pair, shift(pair, "x", -1), shift(pair, "x", 2), shift(pair, "x", 1)], axis=0
    )
    turn = (x + jnp.arange(NX)) % NX
    slot_section = (turn[:, None] * NC + jnp.arange(NC)[None, :]).reshape(-1)
    slot_base, slot_count = base[slot_section], count[slot_section]
    slot_row = jnp.where(slot[None, :] < slot_count[:, None], slot_base[:, None] + slot[None, :], -1)
    slot_row = slot_row.reshape(-1)
    compact = (slot_row[None, :] == row[:, None]).astype(bf16)
    rows = jnp.dot(compact, slots, preferred_element_type=f32)

    gain_half = lax.dynamic_slice_in_dim(norm_gain, c * HALF, HALF)
    sq = jnp.sum(rows * rows, axis=1).reshape(3, HALF)
    hi = sq.astype(bf16)
    mid = (sq - hi.astype(f32)).astype(bf16)
    low = (sq - hi.astype(f32) - mid.astype(f32)).astype(bf16)
    slab = jnp.concatenate(
        [(rows * gain_half[None, :]).astype(bf16), hi, mid, low, jnp.zeros((7, HALF), bf16)],
        axis=0,
    )[None]

    near = jnp.concatenate([slab, send_a(slab, -1), send_a(slab, 2), send_a(slab, 1)], axis=0)
    add = functools.partial(add_logits, table, head_weight, other)

    def places(db):
        return [db % NB * NA + k for k in range(NA)]

    got = {0: near}
    part = add([near], places(0), None)
    up = down = near
    for step in range(1, NB // 2):
        up, down = send_b(up, 1), send_b(down, -1)
        got[NB - step], got[step] = up, down
        part = add([down, up], places(step) + places(-step), part)
    far = [send_b(up[:2], 1), send_b(down[2:], -1)]
    part = add(far, places(NB // 2), part)
    acts = jnp.concatenate([got[k] for k in range(4)] + far + [got[k] for k in range(5, 8)], axis=0)
    other_acts = swap(acts)

    width = NV * VDEV
    start = (section * NV + y * NZ + z) * VDEV
    starts = jnp.stack([start, start + (1 - 2 * c) * width]).astype(jnp.int32)
    logits, stats = softmax_parts(starts, label_col, part, swap(part))
    for axis in ("x", "y", "z"):
        stats = merge(stats, axis)
    top, total, moment, picked, inverse = (stats[k] for k in range(5))
    mean_loss = jnp.sum(top + jnp.log(total) - picked) / EXITS
    inner = row_weight * ((top - picked) + moment / total) / (inverse * D)
    dl_own, dl_got, dl_scaled = logit_gradients(starts, label_col, weight_col, logits, stats)

    grad = functools.partial(gradient_blocks, table, head_weight, other, dl_own, dl_got)
    up, down = grad(places(NB // 2), (2, 2))
    for step in range(NB // 2 - 1, 0, -1):
        up, down = send_b(up, 1), send_b(down, -1)
        a, b = grad(places(step) + places(-step), (4, 4))
        if step == NB // 2 - 1:
            up = jnp.concatenate([a[:2] + up, a[2:]], axis=0)
            down = jnp.concatenate([b[:2], b[2:] + down], axis=0)
        else:
            up, down = a + up, b + down
    up, down = send_b(up, 1), send_b(down, -1)
    (own,) = grad(places(0), (4,))
    summed = own.astype(f32) + (up.astype(f32) + down.astype(f32))
    away = summed.astype(bf16)
    grads = tree(
        [summed[0]]
        + [
            q.astype(f32)
            for q in (send_a(away[3], -1), send_a(away[2], 2), send_a(away[1], 1))
        ]
    )

    d_head = head_gradient(where, acts, other_acts, dl_scaled)

    gain_part = jnp.sum(grads * rows * inverse[:, None], axis=0)
    gain_hi = gain_part.astype(bf16)
    gain_mid = (gain_part - gain_hi.astype(f32)).astype(bf16)
    gain_low = (gain_part - gain_hi.astype(f32) - gain_mid.astype(f32)).astype(bf16)
    tail = jnp.concatenate(
        [gain_hi[None], gain_mid[None], gain_low[None], jnp.zeros((13, HALF), bf16)], axis=0
    )
    expand = (slot_row[:, None] == row[None, :]).astype(bf16)
    spread = jnp.dot(expand, grads.astype(bf16), preferred_element_type=f32).astype(bf16)
    spread = spread.reshape(NX, NC * CAP, HALF)
    packs = [jnp.concatenate([spread[k], tail], axis=0) for k in range(NX)]
    parts = [packs[0], shift(packs[3], "x", -1), shift(packs[2], "x", 2), shift(packs[1], "x", 1)]
    joined = tree([p.astype(f32) for p in parts])
    gain_sum = joined[NC * CAP] + joined[NC * CAP + 1] + joined[NC * CAP + 2]
    by_core = joined[: NC * CAP].reshape(NC, CAP, HALF)
    keep = lax.dynamic_index_in_dim(by_core, c, 0, keepdims=False)
    give = lax.dynamic_index_in_dim(by_core, 1 - c, 0, keepdims=False)
    keep = jnp.concatenate([keep, jnp.broadcast_to(gain_sum[None], (8, HALF))], axis=0)
    give = jnp.concatenate([give, jnp.broadcast_to(gain_sum[None], (8, HALF))], axis=0)
    came = swap(give)
    joint = jnp.concatenate([jnp.where(c == 0, keep, came), jnp.where(c == 0, came, keep)], axis=1)
    d_normed, d_gain = joint[:CAP], joint[CAP]

    own_base = lax.dynamic_index_in_dim(base, section, 0, keepdims=False)
    own_inverse = lax.dynamic_slice_in_dim(jnp.pad(inverse, (0, CAP)), own_base, CAP)
    own_inner = lax.dynamic_slice_in_dim(jnp.pad(inner, (0, CAP)), own_base, CAP)
    scaled = d_normed * norm_gain[None, :]
    d_rows = own_inverse[:, None] * scaled - rows_own.astype(f32) * (
        own_inverse * own_inverse * own_inverse * own_inner
    )[:, None]
    d_hidden = lax.dot_general(
        own_hit, d_rows.astype(bf16), (((0,), (0,)), ((), ())), preferred_element_type=f32
    ).astype(bf16)
    return (mean_loss, d_hidden, d_gain, d_head)


def solution(mesh):
    fine = Mesh(mesh.devices.reshape(NX, NC, NY, NZ), AXES)
    s, v = ("x", "core"), ("y", "z")
    return jax.shard_map(
        body,
        mesh=fine,
        in_specs=(P(s, v), P(v), P(None, AXES), P(), P(), P()),
        out_specs=(P(), P(s, v), P(v), P(None, AXES)),
        check_vma=False,
    )
```

```python
import functools

import jax
import jax.numpy as jnp
import numpy as np
from jax import lax
from jax.experimental import pallas as pl
from jax.experimental.pallas import tpu as pltpu
from jax.sharding import Mesh, PartitionSpec as P

D = 8192
CAP = 96
EXITS = 384
NX, NC, NY, NZ = 4, 2, 4, 8
NV = NY * NZ
NA, NB = 4, 4
AXES = ("x", "core", "y", "z")
HALF = 128
VDEV = 384
ROWS = EXITS + 16
PACK = NC * CAP + 16

epsilon = 1e-05
f32 = jnp.float32
bf16 = jnp.bfloat16
VMEM_BYTES = 32 * 1024 * 1024

STEPS = (0, 1, -1, 2, -2, 3, -3, 4)


def begins(core, x, y):
    return (y + x) % NY if core == 0 else y


TABLE = np.zeros((NC, NX, NY, NZ, NV), np.int32)
for _core, _x, _y, _z, _r in np.ndindex(*TABLE.shape):
    _on = _r // NZ
    _ty = begins(_core, (_x + _on) % NX, _y) if _core == 0 else (_y + _on) % NY
    TABLE[_core, _x, _y, _z, _r] = _ty * NZ + (_z + STEPS[_r % NZ]) % NZ


def move(value, where):
    pairs = []
    for x, core, y in np.ndindex(NX, NC, NY):
        tx, tcore, ty = where(x, core, y)
        pairs.append(((x * NC + core) * NY + y, ((tx % NX) * NC + tcore) * NY + ty % NY))
    return lax.ppermute(value, ("x", "core", "y"), pairs)


def send(value, step):
    return move(
        value, lambda x, core, y: (x + step, core, y) if core == 0 else (x, core, y + step)
    )


def fetch(value, k):
    def where(x, core, y):
        tx = (x - k) % NX
        return tx, core, (y - tx if core == 0 else y)

    return move(value, where)


def deliver(value, k):
    return move(value, lambda x, core, y: (x + k, core, begins(core, x, y)))


def shift(value, axis, step):
    n = {"x": NX, "y": NY, "z": NZ}[axis]
    return lax.ppermute(value, axis, [(i, (i + step) % n) for i in range(n)])


def swap(value):
    return lax.ppermute(value, "core", [(0, 1), (1, 0)])


def tree(parts):
    parts = list(parts)
    while len(parts) > 1:
        h = len(parts) // 2
        parts = [parts[i] + parts[i + h] for i in range(h)]
    return parts[0]


def merge(stats, axis):
    if axis != "z":
        parts = [stats, shift(stats, axis, -1), shift(stats, axis, 2), shift(stats, axis, 1)]
    else:
        down, up = shift(stats, axis, -1), shift(stats, axis, 1)
        near = jnp.concatenate([up, stats, down], axis=0)
        high, low = shift(near, axis, -3), shift(near[8:], axis, 3)
        high, low = high.reshape(3, 8, -1), low.reshape(2, 8, -1)
        parts = [stats, down, high[0], high[1], high[2], low[0], low[1], up]
    peak = parts[0][0]
    for p in parts[1:]:
        peak = jnp.maximum(peak, p[0])
    rows = []
    for p in parts:
        gap = p[0] - peak
        scale = jnp.exp(gap)
        rows.append(jnp.stack([p[1] * scale, scale * (p[2] + p[1] * gap), p[3]]))
    return jnp.concatenate([peak[None], tree(rows), stats[4:]], axis=0)


def whole(shape):
    return pl.BlockSpec(shape, lambda i, t: (0,) * len(shape))


def params(size=VMEM_BYTES):
    return pltpu.CompilerParams(vmem_limit_bytes=size, dimension_semantics=("arbitrary",))


def cost(flops, moved):
    return pl.CostEstimate(flops=flops, bytes_accessed=moved, transcendentals=0)


def split_weights(tables, head_weight, which):
    def kernel(t, head, out):
        c = t[2 * NV]
        side = c if which == 0 else 1 - c

        def copy(r, carry):
            at = pl.multiple_of((t[which * NV + r] * NC + side) * HALF, HALF)
            to = pl.multiple_of(r * HALF, HALF)
            out[pl.ds(to, HALF), :] = head[pl.ds(at, HALF), :]
            return carry

        lax.fori_loop(0, NV, copy, 0)

    return pl.pallas_call(
        kernel,
        out_shape=jax.ShapeDtypeStruct((D // 2, VDEV), bf16),
        grid_spec=pltpu.PrefetchScalarGridSpec(
            num_scalar_prefetch=1,
            grid=(1,),
            in_specs=[whole((D, VDEV))],
            out_specs=whole((D // 2, VDEV)),
        ),
        compiler_params=params(),
        cost_estimate=cost(0, 9_400_000),
        name="split_weights",
    )(tables, head_weight)


def weight_specs(rounds):
    return [
        pl.BlockSpec((NA * HALF, VDEV), lambda i, t, q=q: (q, 0)) for _ in range(2) for q in rounds
    ]


def add_logits(table, weights, rounds, blocks, before):
    n, m = len(rounds), len(blocks)
    first = before is None
    spots = [q * NA + k for q in rounds for k in range(NA)]

    def kernel(t, *refs):
        sides = refs[:n], refs[n : 2 * n]
        acts, rest = refs[2 * n : 2 * n + m], refs[2 * n + m :]
        out, kept, sems = rest[-3:]
        slabs = [(ref, k) for ref in acts for k in range(ref.shape[0])]
        copies = [
            pltpu.make_async_copy(ref.at[k], kept.at[t[spots[i]]], sems.at[i])
            for i, (ref, k) in enumerate(slabs)
        ]
        for copy in copies:
            copy.start()
        squares = sum(ref[k, EXITS:].astype(f32) for ref, k in slabs)
        tail = jnp.concatenate([squares, jnp.zeros((16, 2 * VDEV - HALF), f32)], axis=1)
        lefts = [
            jnp.concatenate([ref[k, :EXITS] for ref, k in slabs[i * NA : (i + 1) * NA]], axis=1)
            for i in range(n)
        ]
        for side, ws in enumerate(sides):
            at = side * VDEV
            value = None if first else rest[0][:EXITS, at : at + VDEV]
            for left, w in zip(lefts, ws, strict=True):
                more = jnp.dot(left, w[...], preferred_element_type=f32)
                value = more if value is None else value + more
            out[:EXITS, at : at + VDEV] = value
        if not first:
            tail += rest[0][EXITS:, :]
        out[EXITS:, :] = tail
        for copy in copies:
            copy.wait()

    anywhere = pl.BlockSpec(memory_space=pl.ANY)
    own, other = weights
    return pl.pallas_call(
        kernel,
        out_shape=(
            jax.ShapeDtypeStruct((ROWS, 2 * VDEV), f32),
            jax.ShapeDtypeStruct((NV, ROWS, HALF), bf16),
        ),
        grid_spec=pltpu.PrefetchScalarGridSpec(
            num_scalar_prefetch=1,
            grid=(1,),
            in_specs=weight_specs(rounds)
            + [whole(b.shape) for b in blocks]
            + ([] if first else [whole((ROWS, 2 * VDEV)), anywhere]),
            out_specs=(whole((ROWS, 2 * VDEV)), anywhere),
            scratch_shapes=[pltpu.SemaphoreType.DMA((n * NA,))],
        ),
        input_output_aliases={} if first else {2 + 2 * n + m: 1},
        compiler_params=params(),
        cost_estimate=cost(2 * EXITS * HALF * n * NA * 2 * VDEV, 2_000_000 * n + 2_400_000),
        name="add_logits",
    )(table, *[own] * n, *[other] * n, *blocks, *([] if first else before))


CONTRACT = (((1,), (1,)), ((), ()))


def products(a, b, own, got):
    value = lax.dot_general(a, own[...], CONTRACT, preferred_element_type=f32)
    value += lax.dot_general(b, got[...], CONTRACT, preferred_element_type=f32)
    return [value[:, k * HALF : (k + 1) * HALF] for k in range(NA)]


def gradient_blocks(table, weights, dl_own, dl_got, rounds):
    n = len(rounds)

    def kernel(t, *refs):
        own, got = refs[:n], refs[n : 2 * n]
        a, b = refs[2 * n][...], refs[2 * n + 1][...]
        outs = refs[2 * n + 2 :]
        for i in range(n):
            value = products(a, b, own[i], got[i])
            for k in range(NA):
                outs[i][k] = value[k].astype(bf16)

    block = jax.ShapeDtypeStruct((NA, EXITS, HALF), bf16)
    own, other = weights
    return pl.pallas_call(
        kernel,
        out_shape=(block,) * n,
        grid_spec=pltpu.PrefetchScalarGridSpec(
            num_scalar_prefetch=1,
            grid=(1,),
            in_specs=weight_specs(rounds) + [whole((EXITS, VDEV))] * 2,
            out_specs=(whole(block.shape),) * n,
        ),
        compiler_params=params(),
        cost_estimate=cost(2 * EXITS * HALF * n * NA * 2 * VDEV, 1_200_000 * n),
        name="gradient_blocks",
    )(table, *[own] * n, *[other] * n, dl_own, dl_got)


def eye():
    shape = (HALF, HALF)
    return lax.broadcasted_iota(jnp.int32, shape, 0) == lax.broadcasted_iota(jnp.int32, shape, 1)


def to_column(row):
    same = eye()
    return jnp.concatenate(
        [
            jnp.sum(jnp.where(same, row[:, k : k + HALF], 0.0), axis=1, keepdims=True)
            for k in range(0, EXITS, HALF)
        ],
        axis=0,
    )


def to_row(column):
    same = eye()
    return jnp.concatenate(
        [
            jnp.sum(jnp.where(same, column[k : k + HALF], 0.0), axis=0, keepdims=True)
            for k in range(0, EXITS, HALF)
        ],
        axis=1,
    )


def softmax_parts(starts, labels, part, got):
    def kernel(starts, lab, part, got, logits, stats):
        sq = part[EXITS:, :HALF] + got[EXITS:, :HALF]
        sq = sq[0:3] + sq[3:6] + sq[6:9]
        sq = jnp.concatenate([sq[0:1], sq[1:2], sq[2:3]], axis=1)
        inverse = lax.rsqrt(to_column(sq) / D + epsilon)
        label = to_column(lab[...]).astype(jnp.int32)
        sides = []
        for side in range(2):
            a, b = side * VDEV, (1 - side) * VDEV
            value = (part[:EXITS, a : a + VDEV] + got[:EXITS, b : b + VDEV]) * inverse
            logits[:, a : a + VDEV] = value
            sides.append(value)
        peak = jnp.maximum(
            jnp.max(sides[0], axis=1, keepdims=True), jnp.max(sides[1], axis=1, keepdims=True)
        )
        sums = []
        for side, value in enumerate(sides):
            gap = value - peak
            power = jnp.exp(gap)
            ids = lax.broadcasted_iota(jnp.int32, (EXITS, VDEV), 1) + starts[side]
            hit = jnp.where(ids == label, value, 0.0)
            sums.append(
                [jnp.sum(q, axis=1, keepdims=True) for q in (power, power * gap, hit)]
            )
        cols = [peak] + [p + q for p, q in zip(*sums, strict=True)] + [inverse]
        rows = [to_row(q) for q in cols] + [jnp.zeros((3, EXITS), f32)]
        stats[...] = jnp.concatenate(rows, axis=0)

    return pl.pallas_call(
        kernel,
        out_shape=(
            jax.ShapeDtypeStruct((EXITS, 2 * VDEV), f32),
            jax.ShapeDtypeStruct((8, EXITS), f32),
        ),
        grid_spec=pltpu.PrefetchScalarGridSpec(
            num_scalar_prefetch=1,
            grid=(1,),
            in_specs=[whole((1, EXITS)), whole((ROWS, 2 * VDEV)), whole((ROWS, 2 * VDEV))],
            out_specs=(whole((EXITS, 2 * VDEV)), whole((8, EXITS))),
        ),
        compiler_params=params(),
        cost_estimate=cost(3_000_000, 3_700_000),
        name="softmax_parts",
    )(starts, labels, part, got)


def logit_gradients(starts, labels, weight, logits, stats, weights, rounds):
    def kernel(starts, lab, w, logits, stats, *refs):
        n = len(rounds)
        owns, gots, (dl_own, dl_got, scaled), outs = (
            refs[:n],
            refs[n : 2 * n],
            refs[2 * n : 2 * n + 3],
            refs[2 * n + 3 :],
        )
        logsum = to_column(stats[0:1] + jnp.log(stats[1:2]))
        inverse, label, scale = to_column(stats[4:5]), to_column(lab[...]).astype(jnp.int32), to_column(w[...])
        parts = []
        for side, out in ((0, dl_own), (1, dl_got)):
            a = side * VDEV
            soft = jnp.exp(logits[:, a : a + VDEV] - logsum)
            ids = lax.broadcasted_iota(jnp.int32, (EXITS, VDEV), 1) + starts[side]
            value = scale * (soft - jnp.where(ids == label, 1.0, 0.0))
            part = value.astype(bf16)
            out[...] = part
            parts.append(part)
            if side == 0:
                scaled[...] = (value * inverse).astype(bf16)
        for own, got, ref in zip(owns, gots, outs, strict=True):
            value = products(*parts, own, got)
            for k in range(NA):
                ref[k] = value[k].astype(bf16)

    far = jax.ShapeDtypeStruct((NA, EXITS, HALF), bf16)
    own, other = weights
    return pl.pallas_call(
        kernel,
        out_shape=tuple(jax.ShapeDtypeStruct((EXITS, VDEV), bf16) for _ in range(3)) + (far,) * len(rounds),
        grid_spec=pltpu.PrefetchScalarGridSpec(
            num_scalar_prefetch=1,
            grid=(1,),
            in_specs=[
                whole((1, EXITS)),
                whole((1, EXITS)),
                whole((EXITS, 2 * VDEV)),
                whole((8, EXITS)),
            ]
            + weight_specs(rounds),
            out_specs=tuple(whole((EXITS, VDEV)) for _ in range(3))
            + (whole(far.shape),) * len(rounds),
        ),
        compiler_params=params(),
        cost_estimate=cost(300_000_000, 3_500_000),
        name="logit_gradients",
    )(starts, labels, weight, logits, stats, *[own] * len(rounds), *[other] * len(rounds))


def head_gradient(core, own, got, dl, part, parts, before):
    per = 4
    steps = NV // per // parts
    first = before is None

    def kernel(t, p, q, d, *rest):
        out = rest[-1]
        for ref, side in ((p, t[0]), (q, 1 - t[0])):
            left = jnp.concatenate([ref[k] for k in range(per)], axis=1)
            value = lax.dot_general(
                left, d[...], (((0,), (0,)), ((), ())), preferred_element_type=f32
            ).astype(bf16)
            for k in range(per):
                at = pl.multiple_of(2 * k * HALF + side * HALF, HALF)
                out[pl.ds(at, HALF), :] = value[k * HALF : (k + 1) * HALF]

    block = pl.BlockSpec((per, EXITS, HALF), lambda i, t: (i + part * steps, 0, 0))
    return pl.pallas_call(
        kernel,
        out_shape=jax.ShapeDtypeStruct((D, VDEV), bf16),
        grid_spec=pltpu.PrefetchScalarGridSpec(
            num_scalar_prefetch=1,
            grid=(steps,),
            in_specs=[block, block, whole((EXITS, VDEV))]
            + ([] if first else [pl.BlockSpec(memory_space=pl.ANY)]),
            out_specs=pl.BlockSpec((2 * HALF * per, VDEV), lambda i, t: (i + part * steps, 0)),
        ),
        input_output_aliases={} if first else {4: 0},
        compiler_params=params(),
        cost_estimate=cost(2 * EXITS * D * VDEV // parts, 13_000_000 // parts),
        name="head_gradient",
    )(core, own, got, dl, *([] if first else [before]))


def row_tables(mask, targets, section_weight):
    def kernel(mask, targets, weight, table, labels, weights):
        row = lax.broadcasted_iota(jnp.int32, (EXITS, 1), 0).astype(f32)
        upper = lax.broadcasted_iota(jnp.int32, (256, 256), 0) <= lax.broadcasted_iota(
            jnp.int32, (256, 256), 1
        )
        upper = upper.astype(bf16)
        label = jnp.zeros((EXITS, 1), f32)
        scale = jnp.zeros((EXITS, 1), f32)
        base = jnp.int32(0)
        for s in range(NX * NC):
            m = mask[:, s * 256 : (s + 1) * 256]
            number = jnp.sum(m)
            table[s], table[8 + s] = base, number
            live = jnp.broadcast_to(m.astype(f32), (8, 256)).astype(bf16)
            rank = jnp.dot(live, upper, preferred_element_type=f32)[0:1]
            place = jnp.where(m == 1, rank + (base - 1).astype(f32), -1.0)
            goal = targets[:, s * 256 : (s + 1) * 256].astype(f32)
            label += jnp.sum(jnp.where(place == row, goal, 0.0), axis=1, keepdims=True)
            at = row - base.astype(f32)
            scale += jnp.where((at >= 0.0) & (at < number.astype(f32)), weight[s], 0.0)
            base = base + number
        labels[...] = to_row(label)
        weights[...] = to_row(scale)

    vmem, smem = pl.BlockSpec(memory_space=pltpu.VMEM), pl.BlockSpec(memory_space=pltpu.SMEM)
    return pl.pallas_call(
        kernel,
        out_shape=(
            jax.ShapeDtypeStruct((16,), jnp.int32),
            jax.ShapeDtypeStruct((1, EXITS), f32),
            jax.ShapeDtypeStruct((1, EXITS), f32),
        ),
        in_specs=[vmem, vmem, smem],
        out_specs=(smem, vmem, vmem),
        cost_estimate=cost(4_000_000, 500_000),
        name="row_tables",
    )(mask, targets, section_weight)


def sum_blocks(*blocks):
    def kernel(*refs):
        ins, outs = refs[:6], refs[6:]
        for i in range(2):
            own, left, right = ins[3 * i : 3 * i + 3]
            for k in range(NA):
                value = own[k].astype(f32) + (left[k].astype(f32) + right[k].astype(f32))
                outs[i * NA + k][0] = value.astype(bf16)

    return pl.pallas_call(
        kernel,
        out_shape=tuple(jax.ShapeDtypeStruct((1, EXITS, HALF), bf16) for _ in range(NZ)),
        cost_estimate=cost(1_000_000, 3_200_000),
        name="sum_blocks",
    )(*blocks[0], *blocks[1])


def thirds(value):
    hi = value.astype(bf16).astype(f32)
    mid = (value - hi).astype(bf16).astype(f32)
    low = value - hi - mid
    pad = jnp.zeros((16 - 3 * value.shape[0], HALF), f32)
    return jnp.concatenate([hi, mid, low, pad], axis=0).astype(bf16)


def select_rows(mask, gain, hidden):
    def kernel(mask, gain, hidden, hit, rows, keep, give):
        x, c = lax.axis_index("x"), lax.axis_index("core")
        upper = lax.broadcasted_iota(jnp.int32, (256, 256), 0) <= lax.broadcasted_iota(
            jnp.int32, (256, 256), 1
        )
        m = mask[:, pl.ds(pl.multiple_of((x * NC + c) * 256, 256), 256)]
        live = jnp.broadcast_to(m.astype(f32), (8, 256)).astype(bf16)
        rank = jnp.dot(live, upper.astype(bf16), preferred_element_type=f32)[0:1]
        place = jnp.where(m == 1, rank - 1.0, -1.0)
        slot = lax.broadcasted_iota(jnp.int32, (CAP, 1), 0).astype(f32)
        chosen = jnp.where(place == slot, 1.0, 0.0).astype(bf16)
        hit[...] = chosen
        value = jnp.dot(chosen, hidden[...], preferred_element_type=f32).astype(bf16)
        rows[...] = value
        first = c == 0
        left, right = value[:, :HALF], value[:, HALF:]
        keep[:CAP, :] = jnp.where(first, left, right)
        give[...] = jnp.where(first, right, left)
        keep[CAP:, :] = thirds(jnp.where(first, gain[0:1], gain[1:2]))

    return pl.pallas_call(
        kernel,
        out_shape=(
            jax.ShapeDtypeStruct((CAP, 256), bf16),
            jax.ShapeDtypeStruct((CAP, 256), bf16),
            jax.ShapeDtypeStruct((CAP + 16, HALF), bf16),
            jax.ShapeDtypeStruct((CAP, HALF), bf16),
        ),
        cost_estimate=cost(20_000_000, 300_000),
        name="select_rows",
    )(mask, gain, hidden)


def compact_rows(table, pairs_of):
    def kernel(t, p0, p1, p2, p3, rows, slab):
        at = lax.broadcasted_iota(jnp.int32, (EXITS, CAP), 0)
        slot = lax.broadcasted_iota(jnp.int32, (EXITS, CAP), 1)
        x, c = lax.axis_index("x"), lax.axis_index("core")
        total = jnp.zeros((EXITS, HALF), f32)
        for k, ref in enumerate((p0, p1, p2, p3)):
            for j in range(NC):
                s = lax.rem(x + k, NX) * NC + (c if j == 0 else 1 - c)
                hit = (at - slot == t[s]) & (slot < t[8 + s])
                hit = jnp.where(hit, 1.0, 0.0).astype(bf16)
                first = j * (CAP + 16)
                total += jnp.dot(hit, ref[first : first + CAP, :], preferred_element_type=f32)
        rows[...] = total.astype(bf16)
        scale = p0[CAP : CAP + 16, :].astype(f32)
        scale = scale[0:1] + scale[1:2] + scale[2:3]
        slab[0, :EXITS, :] = (total * scale).astype(bf16)
        sq = to_row(jnp.sum(total * total, axis=1, keepdims=True))
        sq = jnp.concatenate([sq[:, k : k + HALF] for k in range(0, EXITS, HALF)], axis=0)
        slab[0, EXITS:, :] = thirds(sq)

    return pl.pallas_call(
        kernel,
        out_shape=(
            jax.ShapeDtypeStruct((EXITS, HALF), bf16),
            jax.ShapeDtypeStruct((1, ROWS, HALF), bf16),
        ),
        grid_spec=pltpu.PrefetchScalarGridSpec(
            num_scalar_prefetch=1,
            grid=(1,),
            in_specs=[whole((PACK, HALF))] * NX,
            out_specs=(whole((EXITS, HALF)), whole((1, ROWS, HALF))),
        ),
        cost_estimate=cost(80_000_000, 500_000),
        name="compact_rows",
    )(table, *pairs_of)


def spread_rows(table, inverse, rows, parts):
    def kernel(t, inverse, rows, *refs):
        outs = refs[NZ:]
        grads = tree([ref[0].astype(f32) for ref in refs[:NZ]])
        inv = to_column(inverse[...])
        gain = jnp.sum(grads * rows[...].astype(f32) * inv, axis=0, keepdims=True)
        tail = thirds(gain)
        slot = lax.broadcasted_iota(jnp.int32, (CAP, EXITS), 0)
        at = lax.broadcasted_iota(jnp.int32, (CAP, EXITS), 1)
        x, c = lax.axis_index("x"), lax.axis_index("core")
        value = grads.astype(bf16)
        for k, ref in enumerate(outs):
            for j in range(NC):
                s = lax.rem(x + k, NX) * NC + (c if j == 0 else 1 - c)
                hit = (at - slot == t[s]) & (slot < t[8 + s])
                hit = jnp.where(hit, 1.0, 0.0).astype(bf16)
                ref[j * CAP : (j + 1) * CAP, :] = jnp.dot(
                    hit, value, preferred_element_type=f32
                ).astype(bf16)
            ref[NC * CAP :, :] = tail

    shape = (PACK, HALF)
    return pl.pallas_call(
        kernel,
        out_shape=tuple(jax.ShapeDtypeStruct(shape, bf16) for _ in range(NX)),
        grid_spec=pltpu.PrefetchScalarGridSpec(
            num_scalar_prefetch=1,
            grid=(1,),
            in_specs=[whole((1, EXITS)), whole((EXITS, HALF))] + [whole((1, EXITS, HALF))] * NZ,
            out_specs=tuple(whole(shape) for _ in range(NX)),
        ),
        cost_estimate=cost(80_000_000, 700_000),
        name="spread_rows",
    )(table, inverse, rows, *parts)


def together(*values):
    return lax.optimization_barrier(values)


def after(value, *others):
    return lax.optimization_barrier((value, *others))[0]


def body(hidden, norm_gain, head_weight, exit_mask, targets, section_weight):
    x, c = lax.axis_index("x").astype(jnp.int32), lax.axis_index("core").astype(jnp.int32)
    y, z = lax.axis_index("y"), lax.axis_index("z")
    section = x * NC + c

    mask = exit_mask.reshape(1, -1)
    own_hit, rows_own, keep, give = select_rows(mask, norm_gain.reshape(NC, HALF), hidden)
    pack = jnp.concatenate([keep, swap(give)], axis=0)
    row_table, labels, row_weight = row_tables(
        after(mask, pack), targets.reshape(1, -1), section_weight
    )
    base = row_table[:8]
    rows, slab = compact_rows(row_table, [fetch(pack, k) for k in range(NX)])

    spots = lax.dynamic_slice(jnp.asarray(TABLE), (0, x, y, z, 0), (NC, 1, 1, 1, NV))
    spots = spots.reshape(NC, NV)
    mine = jnp.where(c == 0, spots[0], spots[1])
    theirs = jnp.where(c == 0, spots[1], spots[0])
    table = jnp.concatenate([mine, theirs, c[None]])

    give = split_weights(after(table, slab), head_weight, 1)
    own_weights = split_weights(after(table, give), head_weight, 0)
    came = [shift(slab, "z", -k) for k in STEPS[1:]]
    *came, give, own_weights = together(*came, give, own_weights)
    near_a = jnp.concatenate([slab] + came[: NA - 1], axis=0)
    near_b = jnp.concatenate(came[NA - 1 :], axis=0)
    left_a, right_b = send(near_a, 1), send(near_b, -1)
    left_b, right_a = send(near_b, 1), send(near_a, -1)
    weights = own_weights, swap(give)
    far_a, far_b = send(left_a, 1), send(right_b, -1)
    add = functools.partial(add_logits, table, weights)
    part = add([0, 1], [near_a, near_b], None)
    left_b, right_a = after(left_b, part[0]), after(right_a, part[0])
    part = add([2, 6, 3, 7], [right_a, left_a, right_b, left_b], part)
    far_a, far_b = after(far_a, part[0]), after(far_b, part[0])
    part, acts = add([4, 5], [far_a, far_b], part)

    width = NV * VDEV
    start = (section * NV + y * NZ + z) * VDEV
    starts = jnp.stack([start, start + (1 - 2 * c) * width]).astype(jnp.int32)
    logits, stats = softmax_parts(starts, labels, part, swap(part))
    other_acts = swap(after(acts, stats))
    for axis in ("x", "y", "z"):
        stats = merge(stats, axis)
    top, total, moment, picked, inverse = (stats[k] for k in range(5))
    mean_loss = jnp.sum(top + jnp.log(total) - picked) / EXITS
    inner = row_weight[0] * ((top - picked) + moment / total) / (inverse * D)
    dl_own, dl_got, dl_scaled, far_a, far_b, right_b, left_a = logit_gradients(
        starts, labels, row_weight, logits, stats, weights, [4, 5, 3, 6]
    )

    grad = functools.partial(gradient_blocks, table, weights, dl_own, dl_got)
    head = functools.partial(head_gradient, c[None], acts, other_acts)
    parts = 4
    come_a, come_b = send(far_a, 1), send(far_b, -1)
    from_left_b, from_right_a = send(right_b, 1), send(left_a, -1)
    right_a, left_b, own_a, own_b = grad([2, 7, 0, 1])
    d_head = head(dl_scaled, 0, parts, None)
    come_a, come_b, from_left_b, from_right_a, d_head = together(
        come_a, come_b, from_left_b, from_right_a, d_head
    )
    right_a, left_b = right_a + come_a, left_b + come_b
    from_left_a, from_right_b = send(right_a, 1), send(left_b, -1)
    d_head = head(after(dl_scaled, right_a, left_b), 1, parts, d_head)
    from_left_a, from_right_b, d_head = together(from_left_a, from_right_b, d_head)

    sums = sum_blocks((own_a, from_left_a, from_right_a), (own_b, from_left_b, from_right_b))
    came = [shift(q, "z", k) for q, k in zip(sums[1:], STEPS[1:], strict=True)]
    d_head = head(after(dl_scaled, sums[0]), 2, parts, d_head)
    *came, d_head = together(*came, d_head)
    packs = spread_rows(row_table, inverse[None], rows, [sums[0]] + came)
    came = [deliver(packs[k], k) for k in range(NX)]
    d_head = head(after(dl_scaled, packs[0]), 3, parts, d_head)
    *came, d_head = together(*came, d_head)
    joined = tree([p.astype(f32) for p in came])
    gain_sum = joined[NC * CAP] + joined[NC * CAP + 1] + joined[NC * CAP + 2]
    keep, give = joined[:CAP], joined[CAP : NC * CAP]
    keep = jnp.concatenate([keep, jnp.broadcast_to(gain_sum[None], (8, HALF))], axis=0)
    give = jnp.concatenate([give, jnp.broadcast_to(gain_sum[None], (8, HALF))], axis=0)
    came = swap(give)
    joint = jnp.concatenate([jnp.where(c == 0, keep, came), jnp.where(c == 0, came, keep)], axis=1)
    d_normed, d_gain = joint[:CAP], joint[CAP]

    own_base = lax.dynamic_index_in_dim(base, section, 0, keepdims=False)
    own_inverse = lax.dynamic_slice_in_dim(jnp.pad(inverse, (0, CAP)), own_base, CAP)
    own_inner = lax.dynamic_slice_in_dim(jnp.pad(inner, (0, CAP)), own_base, CAP)
    scaled = d_normed * norm_gain[None, :]
    d_rows = own_inverse[:, None] * scaled - rows_own.astype(f32) * (
        own_inverse * own_inverse * own_inverse * own_inner
    )[:, None]
    d_hidden = lax.dot_general(
        own_hit, d_rows.astype(bf16), (((0,), (0,)), ((), ())), preferred_element_type=f32
    ).astype(bf16)
    return (mean_loss, d_hidden, d_gain, d_head)


def solution(mesh):
    fine = Mesh(mesh.devices.reshape(NX, NC, NY, NZ), AXES)
    s, v = ("x", "core"), ("y", "z")
    return jax.shard_map(
        body,
        mesh=fine,
        in_specs=(P(s, v), P(v), P(None, AXES), P(), P(), P()),
        out_specs=(P(), P(s, v), P(v), P(None, AXES)),
        check_vma=False,
    )
```

```python
import functools

import jax
import jax.numpy as jnp
import numpy as np
from jax import lax
from jax.experimental import pallas as pl
from jax.experimental.pallas import tpu as pltpu
from jax.sharding import Mesh, PartitionSpec as P

D = 8192
CAP = 96
EXITS = 384
NX, NC, NY, NZ = 4, 2, 4, 8
NV = NY * NZ
NA, NB = 4, 4
AXES = ("x", "core", "y", "z")
HALF = 128
VDEV = 384
ROWS = EXITS + 16
PACK = NC * CAP + 16

epsilon = 1e-05
f32 = jnp.float32
bf16 = jnp.bfloat16
VMEM_BYTES = 32 * 1024 * 1024
MORE_BYTES = 60 * 1024 * 1024

STEPS = (0, 1, -1, 2, -2, 3, -3, 4)


def begins(core, x, y):
    return (y + x) % NY if core == 0 else y


TABLE = np.zeros((NC, NX, NY, NZ, NV), np.int32)
for _core, _x, _y, _z, _r in np.ndindex(*TABLE.shape):
    _on = _r // NZ
    _ty = begins(_core, (_x + _on) % NX, _y) if _core == 0 else (_y + _on) % NY
    TABLE[_core, _x, _y, _z, _r] = _ty * NZ + (_z + STEPS[_r % NZ]) % NZ


def move(value, where):
    pairs = []
    for x, core, y in np.ndindex(NX, NC, NY):
        tx, tcore, ty = where(x, core, y)
        pairs.append(((x * NC + core) * NY + y, ((tx % NX) * NC + tcore) * NY + ty % NY))
    return lax.ppermute(value, ("x", "core", "y"), pairs)


def send(value, step):
    return move(
        value, lambda x, core, y: (x + step, core, y) if core == 0 else (x, core, y + step)
    )


def fetch(value, k):
    def where(x, core, y):
        tx = (x - k) % NX
        return tx, core, (y - tx if core == 0 else y)

    return move(value, where)


def deliver(value, k):
    return move(value, lambda x, core, y: (x + k, core, begins(core, x, y)))


def shift(value, axis, step):
    n = {"x": NX, "y": NY, "z": NZ}[axis]
    return lax.ppermute(value, axis, [(i, (i + step) % n) for i in range(n)])


def swap(value):
    return lax.ppermute(value, "core", [(0, 1), (1, 0)])


def tree(parts):
    parts = list(parts)
    while len(parts) > 1:
        h = len(parts) // 2
        parts = [parts[i] + parts[i + h] for i in range(h)]
    return parts[0]


def merge(stats, axis):
    if axis != "z":
        parts = [stats, shift(stats, axis, -1), shift(stats, axis, 2), shift(stats, axis, 1)]
    else:
        parts = jnp.broadcast_to(stats[None], (NZ, *stats.shape))
        parts = lax.all_to_all(parts, axis, 0, 0, tiled=True)
    peak = parts[0][0]
    for p in parts[1:]:
        peak = jnp.maximum(peak, p[0])
    rows = []
    for p in parts:
        gap = p[0] - peak
        scale = jnp.exp(gap)
        rows.append(jnp.stack([p[1] * scale, scale * (p[2] + p[1] * gap), p[3]]))
    return jnp.concatenate([peak[None], tree(rows), stats[4:]], axis=0)


def whole(shape):
    return pl.BlockSpec(shape, lambda i, t: (0,) * len(shape))


def params(size=VMEM_BYTES):
    return pltpu.CompilerParams(vmem_limit_bytes=size, dimension_semantics=("arbitrary",))


def cost(flops, moved):
    return pl.CostEstimate(flops=flops, bytes_accessed=moved, transcendentals=0)


def split_weights(tables, head_weight, which):
    def kernel(t, head, out):
        c = t[2 * NV]
        side = c if which == 0 else 1 - c

        def copy(r, carry):
            at = pl.multiple_of((t[which * NV + r] * NC + side) * HALF, HALF)
            to = pl.multiple_of(r * HALF, HALF)
            out[pl.ds(to, HALF), :] = head[pl.ds(at, HALF), :]
            return carry

        lax.fori_loop(0, NV, copy, 0)

    return pl.pallas_call(
        kernel,
        out_shape=jax.ShapeDtypeStruct((D // 2, VDEV), bf16),
        grid_spec=pltpu.PrefetchScalarGridSpec(
            num_scalar_prefetch=1,
            grid=(1,),
            in_specs=[whole((D, VDEV))],
            out_specs=whole((D // 2, VDEV)),
        ),
        compiler_params=params(),
        cost_estimate=cost(0, 1_000_000),
        name="split_weights",
    )(tables, head_weight)


def weight_specs(rounds):
    return [
        pl.BlockSpec((NA * HALF, VDEV), lambda i, t, q=q: (q, 0)) for _ in range(2) for q in rounds
    ]


def add_logits(table, weights, rounds, blocks, before):
    n, m = len(rounds), len(blocks)
    first = before is None
    spots = [q * NA + k for q in rounds for k in range(NA)]

    def kernel(t, *refs):
        sides = refs[:n], refs[n : 2 * n]
        acts, rest = refs[2 * n : 2 * n + m], refs[2 * n + m :]
        out, kept, sems = rest[-3:]
        slabs = [(ref, k) for ref in acts for k in range(ref.shape[0])]
        copies = [
            pltpu.make_async_copy(ref.at[k], kept.at[t[spots[i]]], sems.at[i])
            for i, (ref, k) in enumerate(slabs)
        ]
        for copy in copies:
            copy.start()
        squares = sum(ref[k, EXITS:].astype(f32) for ref, k in slabs)
        tail = jnp.concatenate([squares, jnp.zeros((16, 2 * VDEV - HALF), f32)], axis=1)
        lefts = [
            jnp.concatenate([ref[k, :EXITS] for ref, k in slabs[i * NA : (i + 1) * NA]], axis=1)
            for i in range(n)
        ]
        for side, ws in enumerate(sides):
            at = side * VDEV
            value = None if first else rest[0][:EXITS, at : at + VDEV]
            for left, w in zip(lefts, ws, strict=True):
                more = jnp.dot(left, w[...], preferred_element_type=f32)
                value = more if value is None else value + more
            out[:EXITS, at : at + VDEV] = value
        if not first:
            tail += rest[0][EXITS:, :]
        out[EXITS:, :] = tail
        for copy in copies:
            copy.wait()

    anywhere = pl.BlockSpec(memory_space=pl.ANY)
    own, other = weights
    return pl.pallas_call(
        kernel,
        out_shape=(
            jax.ShapeDtypeStruct((ROWS, 2 * VDEV), f32),
            jax.ShapeDtypeStruct((NV, ROWS, HALF), bf16),
        ),
        grid_spec=pltpu.PrefetchScalarGridSpec(
            num_scalar_prefetch=1,
            grid=(1,),
            in_specs=weight_specs(rounds)
            + [whole(b.shape) for b in blocks]
            + ([] if first else [whole((ROWS, 2 * VDEV)), anywhere]),
            out_specs=(whole((ROWS, 2 * VDEV)), anywhere),
            scratch_shapes=[pltpu.SemaphoreType.DMA((n * NA,))],
        ),
        input_output_aliases={} if first else {2 + 2 * n + m: 1},
        compiler_params=params(),
        cost_estimate=cost(2 * EXITS * HALF * n * NA * 2 * VDEV, 2_000_000 * n + 2_400_000),
        name="add_logits",
    )(table, *[own] * n, *[other] * n, *blocks, *([] if first else before))


CONTRACT = (((1,), (1,)), ((), ()))


def products(a, b, own, got):
    value = lax.dot_general(a, own[...], CONTRACT, preferred_element_type=f32)
    value += lax.dot_general(b, got[...], CONTRACT, preferred_element_type=f32)
    return [value[:, k * HALF : (k + 1) * HALF] for k in range(NA)]


def gradient_blocks(table, weights, dl_own, dl_got, rounds):
    n = len(rounds)

    def kernel(t, *refs):
        own, got = refs[:n], refs[n : 2 * n]
        a, b = refs[2 * n][...], refs[2 * n + 1][...]
        outs = refs[2 * n + 2 :]
        for i in range(n):
            value = products(a, b, own[i], got[i])
            for k in range(NA):
                outs[i][k] = value[k].astype(bf16)

    block = jax.ShapeDtypeStruct((NA, EXITS, HALF), bf16)
    own, other = weights
    return pl.pallas_call(
        kernel,
        out_shape=(block,) * n,
        grid_spec=pltpu.PrefetchScalarGridSpec(
            num_scalar_prefetch=1,
            grid=(1,),
            in_specs=weight_specs(rounds) + [whole((EXITS, VDEV))] * 2,
            out_specs=(whole(block.shape),) * n,
        ),
        compiler_params=params(),
        cost_estimate=cost(2 * EXITS * HALF * n * NA * 2 * VDEV, 1_200_000 * n),
        name="gradient_blocks",
    )(table, *[own] * n, *[other] * n, dl_own, dl_got)


def eye():
    shape = (HALF, HALF)
    return lax.broadcasted_iota(jnp.int32, shape, 0) == lax.broadcasted_iota(jnp.int32, shape, 1)


def to_column(row):
    same = eye()
    return jnp.concatenate(
        [
            jnp.sum(jnp.where(same, row[:, k : k + HALF], 0.0), axis=1, keepdims=True)
            for k in range(0, EXITS, HALF)
        ],
        axis=0,
    )


def to_row(column):
    same = eye()
    return jnp.concatenate(
        [
            jnp.sum(jnp.where(same, column[k : k + HALF], 0.0), axis=0, keepdims=True)
            for k in range(0, EXITS, HALF)
        ],
        axis=1,
    )


def softmax_parts(starts, labels, part, got):
    def kernel(starts, lab, part, got, logits, stats):
        sq = part[EXITS:, :HALF] + got[EXITS:, :HALF]
        sq = sq[0:3] + sq[3:6] + sq[6:9]
        sq = jnp.concatenate([sq[0:1], sq[1:2], sq[2:3]], axis=1)
        inverse = lax.rsqrt(to_column(sq) / D + epsilon)
        label = to_column(lab[...]).astype(jnp.int32)
        sides = []
        for side in range(2):
            a, b = side * VDEV, (1 - side) * VDEV
            value = (part[:EXITS, a : a + VDEV] + got[:EXITS, b : b + VDEV]) * inverse
            logits[:, a : a + VDEV] = value
            sides.append(value)
        peak = jnp.maximum(
            jnp.max(sides[0], axis=1, keepdims=True), jnp.max(sides[1], axis=1, keepdims=True)
        )
        sums = []
        for side, value in enumerate(sides):
            gap = value - peak
            power = jnp.exp(gap)
            ids = lax.broadcasted_iota(jnp.int32, (EXITS, VDEV), 1) + starts[side]
            hit = jnp.where(ids == label, value, 0.0)
            sums.append(
                [jnp.sum(q, axis=1, keepdims=True) for q in (power, power * gap, hit)]
            )
        cols = [peak] + [p + q for p, q in zip(*sums, strict=True)] + [inverse]
        rows = [to_row(q) for q in cols] + [jnp.zeros((3, EXITS), f32)]
        stats[...] = jnp.concatenate(rows, axis=0)

    return pl.pallas_call(
        kernel,
        out_shape=(
            jax.ShapeDtypeStruct((EXITS, 2 * VDEV), f32),
            jax.ShapeDtypeStruct((8, EXITS), f32),
        ),
        grid_spec=pltpu.PrefetchScalarGridSpec(
            num_scalar_prefetch=1,
            grid=(1,),
            in_specs=[whole((1, EXITS)), whole((ROWS, 2 * VDEV)), whole((ROWS, 2 * VDEV))],
            out_specs=(whole((EXITS, 2 * VDEV)), whole((8, EXITS))),
        ),
        compiler_params=params(),
        cost_estimate=cost(3_000_000, 3_700_000),
        name="softmax_parts",
    )(starts, labels, part, got)


def logit_gradients(starts, labels, weight, logits, stats, weights, rounds):
    def kernel(starts, lab, w, logits, stats, *refs):
        n = len(rounds)
        owns, gots, (dl_own, dl_got, scaled), outs = (
            refs[:n],
            refs[n : 2 * n],
            refs[2 * n : 2 * n + 3],
            refs[2 * n + 3 :],
        )
        logsum = to_column(stats[0:1] + jnp.log(stats[1:2]))
        inverse, label, scale = to_column(stats[4:5]), to_column(lab[...]).astype(jnp.int32), to_column(w[...])
        parts = []
        for side, out in ((0, dl_own), (1, dl_got)):
            a = side * VDEV
            soft = jnp.exp(logits[:, a : a + VDEV] - logsum)
            ids = lax.broadcasted_iota(jnp.int32, (EXITS, VDEV), 1) + starts[side]
            value = scale * (soft - jnp.where(ids == label, 1.0, 0.0))
            part = value.astype(bf16)
            out[...] = part
            parts.append(part)
            if side == 0:
                scaled[...] = (value * inverse).astype(bf16)
        for own, got, ref in zip(owns, gots, outs, strict=True):
            value = products(*parts, own, got)
            for k in range(NA):
                ref[k] = value[k].astype(bf16)

    far = jax.ShapeDtypeStruct((NA, EXITS, HALF), bf16)
    own, other = weights
    return pl.pallas_call(
        kernel,
        out_shape=tuple(jax.ShapeDtypeStruct((EXITS, VDEV), bf16) for _ in range(3)) + (far,) * len(rounds),
        grid_spec=pltpu.PrefetchScalarGridSpec(
            num_scalar_prefetch=1,
            grid=(1,),
            in_specs=[
                whole((1, EXITS)),
                whole((1, EXITS)),
                whole((EXITS, 2 * VDEV)),
                whole((8, EXITS)),
            ]
            + weight_specs(rounds),
            out_specs=tuple(whole((EXITS, VDEV)) for _ in range(3))
            + (whole(far.shape),) * len(rounds),
        ),
        compiler_params=params(MORE_BYTES),
        cost_estimate=cost(300_000_000, 3_500_000),
        name="logit_gradients",
    )(starts, labels, weight, logits, stats, *[own] * len(rounds), *[other] * len(rounds))


def head_gradient(core, own, got, dl, part, parts, before):
    per = 4
    steps = NV // per // parts
    first = before is None

    def kernel(t, p, q, d, *rest):
        out = rest[-1]
        for ref, side in ((p, t[0]), (q, 1 - t[0])):
            left = jnp.concatenate([ref[k] for k in range(per)], axis=1)
            value = lax.dot_general(
                left, d[...], (((0,), (0,)), ((), ())), preferred_element_type=f32
            ).astype(bf16)
            for k in range(per):
                at = pl.multiple_of(2 * k * HALF + side * HALF, HALF)
                out[pl.ds(at, HALF), :] = value[k * HALF : (k + 1) * HALF]

    block = pl.BlockSpec((per, EXITS, HALF), lambda i, t: (i + part * steps, 0, 0))
    return pl.pallas_call(
        kernel,
        out_shape=jax.ShapeDtypeStruct((D, VDEV), bf16),
        grid_spec=pltpu.PrefetchScalarGridSpec(
            num_scalar_prefetch=1,
            grid=(steps,),
            in_specs=[block, block, whole((EXITS, VDEV))]
            + ([] if first else [pl.BlockSpec(memory_space=pl.ANY)]),
            out_specs=pl.BlockSpec((2 * HALF * per, VDEV), lambda i, t: (i + part * steps, 0)),
        ),
        input_output_aliases={} if first else {4: 0},
        compiler_params=params(MORE_BYTES),
        cost_estimate=cost(2 * EXITS * D * VDEV // parts, 13_000_000 // parts),
        name="head_gradient",
    )(core, own, got, dl, *([] if first else [before]))


def row_tables(mask, targets, section_weight):
    def kernel(mask, targets, weight, table, labels, weights):
        row = lax.broadcasted_iota(jnp.int32, (EXITS, 1), 0).astype(f32)
        upper = lax.broadcasted_iota(jnp.int32, (256, 256), 0) <= lax.broadcasted_iota(
            jnp.int32, (256, 256), 1
        )
        upper = upper.astype(bf16)
        label = jnp.zeros((EXITS, 1), f32)
        scale = jnp.zeros((EXITS, 1), f32)
        base = jnp.int32(0)
        for s in range(NX * NC):
            m = mask[:, s * 256 : (s + 1) * 256]
            number = jnp.sum(m)
            table[s], table[8 + s] = base, number
            live = jnp.broadcast_to(m.astype(f32), (8, 256)).astype(bf16)
            rank = jnp.dot(live, upper, preferred_element_type=f32)[0:1]
            place = jnp.where(m == 1, rank + (base - 1).astype(f32), -1.0)
            goal = targets[:, s * 256 : (s + 1) * 256].astype(f32)
            label += jnp.sum(jnp.where(place == row, goal, 0.0), axis=1, keepdims=True)
            at = row - base.astype(f32)
            scale += jnp.where((at >= 0.0) & (at < number.astype(f32)), weight[s], 0.0)
            base = base + number
        labels[...] = to_row(label)
        weights[...] = to_row(scale)

    vmem, smem = pl.BlockSpec(memory_space=pltpu.VMEM), pl.BlockSpec(memory_space=pltpu.SMEM)
    return pl.pallas_call(
        kernel,
        out_shape=(
            jax.ShapeDtypeStruct((16,), jnp.int32),
            jax.ShapeDtypeStruct((1, EXITS), f32),
            jax.ShapeDtypeStruct((1, EXITS), f32),
        ),
        in_specs=[vmem, vmem, smem],
        out_specs=(smem, vmem, vmem),
        cost_estimate=cost(4_000_000, 500_000),
        name="row_tables",
    )(mask, targets, section_weight)


def sum_blocks(*blocks):
    def kernel(*refs):
        ins, outs = refs[:6], refs[6:]
        for i in range(2):
            own, left, right = ins[3 * i : 3 * i + 3]
            for k in range(NA):
                value = own[k].astype(f32) + (left[k].astype(f32) + right[k].astype(f32))
                outs[i * NA + k][0] = value.astype(bf16)

    return pl.pallas_call(
        kernel,
        out_shape=tuple(jax.ShapeDtypeStruct((1, EXITS, HALF), bf16) for _ in range(NZ)),
        cost_estimate=cost(1_000_000, 3_200_000),
        name="sum_blocks",
    )(*blocks[0], *blocks[1])


def thirds(value):
    hi = value.astype(bf16).astype(f32)
    mid = (value - hi).astype(bf16).astype(f32)
    low = value - hi - mid
    pad = jnp.zeros((16 - 3 * value.shape[0], HALF), f32)
    return jnp.concatenate([hi, mid, low, pad], axis=0).astype(bf16)


def select_rows(mask, gain, hidden):
    def kernel(mask, gain, hidden, hit, rows, keep, give):
        x, c = lax.axis_index("x"), lax.axis_index("core")
        upper = lax.broadcasted_iota(jnp.int32, (256, 256), 0) <= lax.broadcasted_iota(
            jnp.int32, (256, 256), 1
        )
        m = mask[:, pl.ds(pl.multiple_of((x * NC + c) * 256, 256), 256)]
        live = jnp.broadcast_to(m.astype(f32), (8, 256)).astype(bf16)
        rank = jnp.dot(live, upper.astype(bf16), preferred_element_type=f32)[0:1]
        place = jnp.where(m == 1, rank - 1.0, -1.0)
        slot = lax.broadcasted_iota(jnp.int32, (CAP, 1), 0).astype(f32)
        chosen = jnp.where(place == slot, 1.0, 0.0).astype(bf16)
        hit[...] = chosen
        value = jnp.dot(chosen, hidden[...], preferred_element_type=f32).astype(bf16)
        rows[...] = value
        first = c == 0
        left, right = value[:, :HALF], value[:, HALF:]
        keep[:CAP, :] = jnp.where(first, left, right)
        give[...] = jnp.where(first, right, left)
        keep[CAP:, :] = thirds(jnp.where(first, gain[0:1], gain[1:2]))

    return pl.pallas_call(
        kernel,
        out_shape=(
            jax.ShapeDtypeStruct((CAP, 256), bf16),
            jax.ShapeDtypeStruct((CAP, 256), bf16),
            jax.ShapeDtypeStruct((CAP + 16, HALF), bf16),
            jax.ShapeDtypeStruct((CAP, HALF), bf16),
        ),
        cost_estimate=cost(20_000_000, 300_000),
        name="select_rows",
    )(mask, gain, hidden)


def compact_rows(table, pairs_of):
    def kernel(t, p0, p1, p2, p3, rows, slab):
        at = lax.broadcasted_iota(jnp.int32, (EXITS, CAP), 0)
        slot = lax.broadcasted_iota(jnp.int32, (EXITS, CAP), 1)
        x, c = lax.axis_index("x"), lax.axis_index("core")
        total = jnp.zeros((EXITS, HALF), f32)
        for k, ref in enumerate((p0, p1, p2, p3)):
            for j in range(NC):
                s = lax.rem(x + k, NX) * NC + (c if j == 0 else 1 - c)
                hit = (at - slot == t[s]) & (slot < t[8 + s])
                hit = jnp.where(hit, 1.0, 0.0).astype(bf16)
                first = j * (CAP + 16)
                total += jnp.dot(hit, ref[first : first + CAP, :], preferred_element_type=f32)
        rows[...] = total.astype(bf16)
        scale = p0[CAP : CAP + 16, :].astype(f32)
        scale = scale[0:1] + scale[1:2] + scale[2:3]
        slab[0, :EXITS, :] = (total * scale).astype(bf16)
        sq = to_row(jnp.sum(total * total, axis=1, keepdims=True))
        sq = jnp.concatenate([sq[:, k : k + HALF] for k in range(0, EXITS, HALF)], axis=0)
        slab[0, EXITS:, :] = thirds(sq)

    return pl.pallas_call(
        kernel,
        out_shape=(
            jax.ShapeDtypeStruct((EXITS, HALF), bf16),
            jax.ShapeDtypeStruct((1, ROWS, HALF), bf16),
        ),
        grid_spec=pltpu.PrefetchScalarGridSpec(
            num_scalar_prefetch=1,
            grid=(1,),
            in_specs=[whole((PACK, HALF))] * NX,
            out_specs=(whole((EXITS, HALF)), whole((1, ROWS, HALF))),
        ),
        compiler_params=params(MORE_BYTES),
        cost_estimate=cost(80_000_000, 500_000),
        name="compact_rows",
    )(table, *pairs_of)


def spread_rows(table, inverse, rows, parts):
    def kernel(t, inverse, rows, *refs):
        outs = refs[NZ:]
        grads = tree([ref[0].astype(f32) for ref in refs[:NZ]])
        inv = to_column(inverse[...])
        gain = jnp.sum(grads * rows[...].astype(f32) * inv, axis=0, keepdims=True)
        tail = thirds(gain)
        slot = lax.broadcasted_iota(jnp.int32, (CAP, EXITS), 0)
        at = lax.broadcasted_iota(jnp.int32, (CAP, EXITS), 1)
        x, c = lax.axis_index("x"), lax.axis_index("core")
        value = grads.astype(bf16)
        for k, ref in enumerate(outs):
            for j in range(NC):
                s = lax.rem(x + k, NX) * NC + (c if j == 0 else 1 - c)
                hit = (at - slot == t[s]) & (slot < t[8 + s])
                hit = jnp.where(hit, 1.0, 0.0).astype(bf16)
                ref[j * CAP : (j + 1) * CAP, :] = jnp.dot(
                    hit, value, preferred_element_type=f32
                ).astype(bf16)
            ref[NC * CAP :, :] = tail

    shape = (PACK, HALF)
    return pl.pallas_call(
        kernel,
        out_shape=tuple(jax.ShapeDtypeStruct(shape, bf16) for _ in range(NX)),
        grid_spec=pltpu.PrefetchScalarGridSpec(
            num_scalar_prefetch=1,
            grid=(1,),
            in_specs=[whole((1, EXITS)), whole((EXITS, HALF))] + [whole((1, EXITS, HALF))] * NZ,
            out_specs=tuple(whole(shape) for _ in range(NX)),
        ),
        compiler_params=params(MORE_BYTES),
        cost_estimate=cost(80_000_000, 700_000),
        name="spread_rows",
    )(table, inverse, rows, *parts)


def finish(table, stats, weight, gain, keep, came, rows, hit):
    def kernel(t, stats, w, gain, keep, came, rows, hit, hidden, out):
        x, c = lax.axis_index("x"), lax.axis_index("core")
        top, total, moment, picked, inverse = (stats[k : k + 1] for k in range(5))
        inner = w[...] * ((top - picked) + moment / total) / (inverse * D)
        at = lax.broadcasted_iota(jnp.int32, (CAP, EXITS), 1)
        slot = lax.broadcasted_iota(jnp.int32, (CAP, EXITS), 0)
        mine = at - slot == t[x * NC + c]
        inverse, inner = (
            jnp.sum(jnp.where(mine, q, 0.0), axis=1, keepdims=True) for q in (inverse, inner)
        )
        first = c == 0
        left = jnp.where(first, keep[...], came[...])
        right = jnp.where(first, came[...], keep[...])
        grads = jnp.concatenate([left[:CAP], right[:CAP]], axis=1)
        scale = jnp.concatenate([gain[0:1], gain[1:2]], axis=1)
        value = inverse * (grads * scale) - rows[...].astype(f32) * (
            inverse * inverse * inverse * inner
        )
        hidden[...] = lax.dot_general(
            hit[...], value.astype(bf16), (((0,), (0,)), ((), ())), preferred_element_type=f32
        ).astype(bf16)
        out[...] = jnp.concatenate([left[CAP : CAP + 1], right[CAP : CAP + 1]], axis=1)

    return pl.pallas_call(
        kernel,
        out_shape=(
            jax.ShapeDtypeStruct((256, 2 * HALF), bf16),
            jax.ShapeDtypeStruct((1, 2 * HALF), f32),
        ),
        grid_spec=pltpu.PrefetchScalarGridSpec(
            num_scalar_prefetch=1,
            grid=(1,),
            in_specs=[
                whole((8, EXITS)),
                whole((1, EXITS)),
                whole((NC, HALF)),
                whole((CAP + 8, HALF)),
                whole((CAP + 8, HALF)),
                whole((CAP, 2 * HALF)),
                whole((CAP, 256)),
            ],
            out_specs=(whole((256, 2 * HALF)), whole((1, 2 * HALF))),
        ),
        compiler_params=params(),
        cost_estimate=cost(13_000_000, 500_000),
        name="finish",
    )(table, stats, weight, gain, keep, came, rows, hit)


def together(*values):
    return lax.optimization_barrier(values)


def after(value, *others):
    return lax.optimization_barrier((value, *others))[0]


def body(hidden, norm_gain, head_weight, exit_mask, targets, section_weight):
    x, c = lax.axis_index("x").astype(jnp.int32), lax.axis_index("core").astype(jnp.int32)
    y, z = lax.axis_index("y"), lax.axis_index("z")
    section = x * NC + c

    mask = exit_mask.reshape(1, -1)
    own_hit, rows_own, keep, give = select_rows(mask, norm_gain.reshape(NC, HALF), hidden)
    pack = jnp.concatenate([keep, swap(give)], axis=0)
    row_table, labels, row_weight = row_tables(
        after(mask, pack), targets.reshape(1, -1), section_weight
    )
    rows, slab = compact_rows(row_table, [fetch(pack, k) for k in range(NX)])

    spots = lax.dynamic_slice(jnp.asarray(TABLE), (0, x, y, z, 0), (NC, 1, 1, 1, NV))
    spots = spots.reshape(NC, NV)
    mine = jnp.where(c == 0, spots[0], spots[1])
    theirs = jnp.where(c == 0, spots[1], spots[0])
    table = jnp.concatenate([mine, theirs, c[None]])

    give = split_weights(after(table, slab), head_weight, 1)
    came = [shift(slab, "z", -k) for k in STEPS[1:]]
    *came, give = together(*came, give)
    own_weights = split_weights(after(table, give), head_weight, 0)
    near_a = jnp.concatenate([slab, *came[: NA - 1]], axis=0)
    near_b = jnp.concatenate(came[NA - 1 :], axis=0)
    left_a, right_b = send(near_a, 1), send(near_b, -1)
    left_b, right_a = send(near_b, 1), send(near_a, -1)
    weights = own_weights, swap(give)
    far_a, far_b = send(left_a, 1), send(right_b, -1)
    add = functools.partial(add_logits, table, weights)
    part = add([0, 1], [near_a, near_b], None)
    left_b, right_a = after(left_b, part[0]), after(right_a, part[0])
    part = add([2, 6, 3, 7], [right_a, left_a, right_b, left_b], part)
    far_a, far_b = after(far_a, part[0]), after(far_b, part[0])
    part, acts = add([4, 5], [far_a, far_b], part)

    width = NV * VDEV
    start = (section * NV + y * NZ + z) * VDEV
    starts = jnp.stack([start, start + (1 - 2 * c) * width]).astype(jnp.int32)
    logits, stats = softmax_parts(starts, labels, part, swap(part))
    other_acts = swap(after(acts, stats))
    for axis in ("x", "y", "z"):
        stats = merge(stats, axis)
    top, total, _, picked, inverse = (stats[k] for k in range(5))
    mean_loss = jnp.sum(top + jnp.log(total) - picked) / EXITS
    dl_own, dl_got, dl_scaled, far_a, far_b, right_b, left_a = logit_gradients(
        starts, labels, row_weight, logits, stats, weights, [4, 5, 3, 6]
    )

    grad = functools.partial(gradient_blocks, table, weights, dl_own, dl_got)
    head = functools.partial(head_gradient, c[None], acts, other_acts)
    parts = 4
    come_a, come_b = send(far_a, 1), send(far_b, -1)
    from_left_b, from_right_a = send(right_b, 1), send(left_a, -1)
    right_a, left_b, own_a, own_b = grad([2, 7, 0, 1])
    come_a, come_b, from_left_b, from_right_a, right_a, left_b = together(
        come_a, come_b, from_left_b, from_right_a, right_a, left_b
    )
    right_a, left_b = right_a + come_a, left_b + come_b
    from_left_a, from_right_b = send(right_a, 1), send(left_b, -1)
    d_head = head(after(dl_scaled, right_a, left_b), 0, parts, None)
    from_left_a, from_right_b, d_head = together(from_left_a, from_right_b, d_head)

    sums = sum_blocks((own_a, from_left_a, from_right_a), (own_b, from_left_b, from_right_b))
    came = [shift(q, "z", k) for q, k in zip(sums[1:], STEPS[1:], strict=True)]
    d_head = head(after(dl_scaled, sums[0]), 1, parts, d_head)
    d_head = head(dl_scaled, 2, parts, d_head)
    *came, d_head = together(*came, d_head)
    packs = spread_rows(row_table, inverse[None], rows, [sums[0]] + came)
    came = [deliver(packs[k], k) for k in range(NX)]
    d_head = head(after(dl_scaled, packs[0]), 3, parts, d_head)
    *came, d_head = together(*came, d_head)
    joined = tree([p.astype(f32) for p in came])
    gain_sum = joined[NC * CAP] + joined[NC * CAP + 1] + joined[NC * CAP + 2]
    keep, give = joined[:CAP], joined[CAP : NC * CAP]
    keep = jnp.concatenate([keep, jnp.broadcast_to(gain_sum[None], (8, HALF))], axis=0)
    give = jnp.concatenate([give, jnp.broadcast_to(gain_sum[None], (8, HALF))], axis=0)
    d_hidden, d_gain = finish(
        row_table, stats, row_weight, norm_gain.reshape(NC, HALF), keep, swap(give), rows_own, own_hit
    )
    d_gain = d_gain.reshape(-1)
    return (mean_loss, d_hidden, d_gain, d_head)


def solution(mesh):
    fine = Mesh(mesh.devices.reshape(NX, NC, NY, NZ), AXES)
    s, v = ("x", "core"), ("y", "z")
    return jax.shard_map(
        body,
        mesh=fine,
        in_specs=(P(s, v), P(v), P(None, AXES), P(), P(), P()),
        out_specs=(P(), P(s, v), P(v), P(None, AXES)),
        check_vma=False,
    )
```

```python
import functools

import jax
import jax.numpy as jnp
import numpy as np
from jax import lax
from jax.experimental import pallas as pl
from jax.experimental.pallas import tpu as pltpu
from jax.sharding import Mesh, PartitionSpec as P

D = 8192
CAP = 96
EXITS = 384
NX, NC, NY, NZ = 4, 2, 4, 8
NV = NY * NZ
NA, NB = 4, 4
AXES = ("x", "core", "y", "z")
HALF = 128
VDEV = 384
ROWS = EXITS + 16
PACK = NC * CAP + 16

epsilon = 1e-05
f32 = jnp.float32
bf16 = jnp.bfloat16
VMEM_BYTES = 32 * 1024 * 1024
MORE_BYTES = 60 * 1024 * 1024

STEPS = (0, 1, -1, 2, -2, 3, -3, 4)


def begins(core, x, y):
    return (y + x) % NY if core == 0 else y


TABLE = np.zeros((NC, NX, NY, NZ, NV), np.int32)
for _core, _x, _y, _z, _r in np.ndindex(*TABLE.shape):
    _on = _r // NZ
    _ty = begins(_core, (_x + _on) % NX, _y) if _core == 0 else (_y + _on) % NY
    TABLE[_core, _x, _y, _z, _r] = _ty * NZ + (_z + STEPS[_r % NZ]) % NZ
TABLE = np.concatenate([TABLE, TABLE[::-1], np.zeros_like(TABLE[..., :3])], axis=-1)
for _core, _x, _y, _z in np.ndindex(NC, NX, NY, NZ):
    _first = [((_x * NC + q) * NV + _y * NZ + _z) * VDEV for q in (_core, 1 - _core)]
    TABLE[_core, _x, _y, _z, 2 * NV :] = [_core, *_first]


def move(value, where):
    pairs = []
    for x, core, y in np.ndindex(NX, NC, NY):
        tx, tcore, ty = where(x, core, y)
        pairs.append(((x * NC + core) * NY + y, ((tx % NX) * NC + tcore) * NY + ty % NY))
    return lax.ppermute(value, ("x", "core", "y"), pairs)


def send(value, step):
    return move(
        value, lambda x, core, y: (x + step, core, y) if core == 0 else (x, core, y + step)
    )


def fetch(value, k):
    def where(x, core, y):
        tx = (x - k) % NX
        return tx, core, (y - tx if core == 0 else y)

    return move(value, where)


def deliver(value, k):
    return move(value, lambda x, core, y: (x + k, core, begins(core, x, y)))


def shift(value, axis, step):
    n = {"x": NX, "y": NY, "z": NZ}[axis]
    return lax.ppermute(value, axis, [(i, (i + step) % n) for i in range(n)])


def swap(value):
    return lax.ppermute(value, "core", [(0, 1), (1, 0)])


def tree(parts):
    parts = list(parts)
    while len(parts) > 1:
        h = len(parts) // 2
        parts = [parts[i] + parts[i + h] for i in range(h)]
    return parts[0]


def merge(stats, axis):
    if axis != "z":
        parts = [stats, shift(stats, axis, -1), shift(stats, axis, 2), shift(stats, axis, 1)]
    else:
        parts = jnp.broadcast_to(stats[None], (NZ, *stats.shape))
        parts = lax.all_to_all(parts, axis, 0, 0, tiled=True)
    peak = parts[0][0]
    for p in parts[1:]:
        peak = jnp.maximum(peak, p[0])
    rows = []
    for p in parts:
        gap = p[0] - peak
        scale = jnp.exp(gap)
        rows.append(jnp.stack([p[1] * scale, scale * (p[2] + p[1] * gap), p[3]]))
    return jnp.concatenate([peak[None], tree(rows), stats[4:]], axis=0)


def whole(shape):
    return pl.BlockSpec(shape, lambda i, t: (0,) * len(shape))


def params(size=VMEM_BYTES):
    return pltpu.CompilerParams(vmem_limit_bytes=size, dimension_semantics=("arbitrary",))


def cost(flops, moved):
    return pl.CostEstimate(flops=flops, bytes_accessed=moved, transcendentals=0)


def split_weights(tables, head_weight, which):
    def kernel(t, head, out):
        c = t[2 * NV]
        side = c if which == 0 else 1 - c

        def copy(r, carry):
            at = pl.multiple_of((t[which * NV + r] * NC + side) * HALF, HALF)
            to = pl.multiple_of(r * HALF, HALF)
            out[pl.ds(to, HALF), :] = head[pl.ds(at, HALF), :]
            return carry

        lax.fori_loop(0, NV, copy, 0)

    return pl.pallas_call(
        kernel,
        out_shape=jax.ShapeDtypeStruct((D // 2, VDEV), bf16),
        grid_spec=pltpu.PrefetchScalarGridSpec(
            num_scalar_prefetch=1,
            grid=(1,),
            in_specs=[whole((D, VDEV))],
            out_specs=whole((D // 2, VDEV)),
        ),
        compiler_params=params(),
        cost_estimate=cost(0, 1_000_000),
        name="split_weights",
    )(tables, head_weight)


def weight_specs(rounds):
    return [
        pl.BlockSpec((NA * HALF, VDEV), lambda i, t, q=q: (q, 0)) for _ in range(2) for q in rounds
    ]


def add_logits(table, weights, rounds, blocks, before):
    n, m = len(rounds), len(blocks)
    first = before is None
    spots = [q * NA + k for q in rounds for k in range(NA)]

    def kernel(t, *refs):
        sides = refs[:n], refs[n : 2 * n]
        acts, rest = refs[2 * n : 2 * n + m], refs[2 * n + m :]
        out, kept, sems = rest[-3:]
        slabs = [(ref, k) for ref in acts for k in range(ref.shape[0])]
        copies = [
            pltpu.make_async_copy(ref.at[k], kept.at[t[spots[i]]], sems.at[i])
            for i, (ref, k) in enumerate(slabs)
        ]
        for copy in copies:
            copy.start()
        squares = sum(ref[k, EXITS:].astype(f32) for ref, k in slabs)
        tail = jnp.concatenate([squares, jnp.zeros((16, 2 * VDEV - HALF), f32)], axis=1)
        lefts = [
            jnp.concatenate([ref[k, :EXITS] for ref, k in slabs[i * NA : (i + 1) * NA]], axis=1)
            for i in range(n)
        ]
        for side, ws in enumerate(sides):
            at = side * VDEV
            value = None if first else rest[0][:EXITS, at : at + VDEV]
            for left, w in zip(lefts, ws, strict=True):
                more = jnp.dot(left, w[...], preferred_element_type=f32)
                value = more if value is None else value + more
            out[:EXITS, at : at + VDEV] = value
        if not first:
            tail += rest[0][EXITS:, :]
        out[EXITS:, :] = tail
        for copy in copies:
            copy.wait()

    anywhere = pl.BlockSpec(memory_space=pl.ANY)
    own, other = weights
    return pl.pallas_call(
        kernel,
        out_shape=(
            jax.ShapeDtypeStruct((ROWS, 2 * VDEV), f32),
            jax.ShapeDtypeStruct((NV, ROWS, HALF), bf16),
        ),
        grid_spec=pltpu.PrefetchScalarGridSpec(
            num_scalar_prefetch=1,
            grid=(1,),
            in_specs=weight_specs(rounds)
            + [whole(b.shape) for b in blocks]
            + ([] if first else [whole((ROWS, 2 * VDEV)), anywhere]),
            out_specs=(whole((ROWS, 2 * VDEV)), anywhere),
            scratch_shapes=[pltpu.SemaphoreType.DMA((n * NA,))],
        ),
        input_output_aliases={} if first else {2 + 2 * n + m: 1},
        compiler_params=params(),
        cost_estimate=cost(2 * EXITS * HALF * n * NA * 2 * VDEV, 2_000_000 * n + 2_400_000),
        name="add_logits",
    )(table, *[own] * n, *[other] * n, *blocks, *([] if first else before))


CONTRACT = (((1,), (1,)), ((), ()))


def products(a, b, own, got):
    value = lax.dot_general(a, own[...], CONTRACT, preferred_element_type=f32)
    value += lax.dot_general(b, got[...], CONTRACT, preferred_element_type=f32)
    return [value[:, k * HALF : (k + 1) * HALF] for k in range(NA)]


def gradient_blocks(table, weights, dl_own, dl_got, rounds):
    n = len(rounds)

    def kernel(t, *refs):
        own, got = refs[:n], refs[n : 2 * n]
        a, b = refs[2 * n][...], refs[2 * n + 1][...]
        outs = refs[2 * n + 2 :]
        for i in range(n):
            value = products(a, b, own[i], got[i])
            for k in range(NA):
                outs[i][k] = value[k].astype(bf16)

    block = jax.ShapeDtypeStruct((NA, EXITS, HALF), bf16)
    own, other = weights
    return pl.pallas_call(
        kernel,
        out_shape=(block,) * n,
        grid_spec=pltpu.PrefetchScalarGridSpec(
            num_scalar_prefetch=1,
            grid=(1,),
            in_specs=weight_specs(rounds) + [whole((EXITS, VDEV))] * 2,
            out_specs=(whole(block.shape),) * n,
        ),
        compiler_params=params(),
        cost_estimate=cost(2 * EXITS * HALF * n * NA * 2 * VDEV, 1_200_000 * n),
        name="gradient_blocks",
    )(table, *[own] * n, *[other] * n, dl_own, dl_got)


def eye():
    shape = (HALF, HALF)
    return lax.broadcasted_iota(jnp.int32, shape, 0) == lax.broadcasted_iota(jnp.int32, shape, 1)


def to_column(row):
    same = eye()
    return jnp.concatenate(
        [
            jnp.sum(jnp.where(same, row[:, k : k + HALF], 0.0), axis=1, keepdims=True)
            for k in range(0, EXITS, HALF)
        ],
        axis=0,
    )


def to_row(column):
    same = eye()
    return jnp.concatenate(
        [
            jnp.sum(jnp.where(same, column[k : k + HALF], 0.0), axis=0, keepdims=True)
            for k in range(0, EXITS, HALF)
        ],
        axis=1,
    )


def softmax_parts(starts, labels, part, got):
    def kernel(starts, lab, part, got, logits, stats):
        sq = part[EXITS:, :HALF] + got[EXITS:, :HALF]
        sq = sq[0:3] + sq[3:6] + sq[6:9]
        sq = jnp.concatenate([sq[0:1], sq[1:2], sq[2:3]], axis=1)
        inverse = lax.rsqrt(to_column(sq) / D + epsilon)
        label = to_column(lab[...]).astype(jnp.int32)
        sides = []
        for side in range(2):
            a, b = side * VDEV, (1 - side) * VDEV
            value = (part[:EXITS, a : a + VDEV] + got[:EXITS, b : b + VDEV]) * inverse
            logits[:, a : a + VDEV] = value
            sides.append(value)
        peak = jnp.maximum(
            jnp.max(sides[0], axis=1, keepdims=True), jnp.max(sides[1], axis=1, keepdims=True)
        )
        sums = []
        for side, value in enumerate(sides):
            gap = value - peak
            power = jnp.exp(gap)
            ids = lax.broadcasted_iota(jnp.int32, (EXITS, VDEV), 1) + starts[2 * NV + 1 + side]
            hit = jnp.where(ids == label, value, 0.0)
            sums.append(
                [jnp.sum(q, axis=1, keepdims=True) for q in (power, power * gap, hit)]
            )
        cols = [peak] + [p + q for p, q in zip(*sums, strict=True)] + [inverse]
        rows = [to_row(q) for q in cols] + [jnp.zeros((3, EXITS), f32)]
        stats[...] = jnp.concatenate(rows, axis=0)

    return pl.pallas_call(
        kernel,
        out_shape=(
            jax.ShapeDtypeStruct((EXITS, 2 * VDEV), f32),
            jax.ShapeDtypeStruct((8, EXITS), f32),
        ),
        grid_spec=pltpu.PrefetchScalarGridSpec(
            num_scalar_prefetch=1,
            grid=(1,),
            in_specs=[whole((1, EXITS)), whole((ROWS, 2 * VDEV)), whole((ROWS, 2 * VDEV))],
            out_specs=(whole((EXITS, 2 * VDEV)), whole((8, EXITS))),
        ),
        compiler_params=params(),
        cost_estimate=cost(3_000_000, 3_700_000),
        name="softmax_parts",
    )(starts, labels, part, got)


def logit_gradients(starts, labels, weight, logits, stats, weights, rounds):
    def kernel(starts, lab, w, logits, stats, *refs):
        n = len(rounds)
        owns, gots, (dl_own, dl_got, scaled), outs = (
            refs[:n],
            refs[n : 2 * n],
            refs[2 * n : 2 * n + 3],
            refs[2 * n + 3 :],
        )
        logsum = to_column(stats[0:1] + jnp.log(stats[1:2]))
        inverse, label, scale = to_column(stats[4:5]), to_column(lab[...]).astype(jnp.int32), to_column(w[...])
        parts = []
        for side, out in ((0, dl_own), (1, dl_got)):
            a = side * VDEV
            soft = jnp.exp(logits[:, a : a + VDEV] - logsum)
            ids = lax.broadcasted_iota(jnp.int32, (EXITS, VDEV), 1) + starts[2 * NV + 1 + side]
            value = scale * (soft - jnp.where(ids == label, 1.0, 0.0))
            part = value.astype(bf16)
            out[...] = part
            parts.append(part)
            if side == 0:
                scaled[...] = (value * inverse).astype(bf16)
        for own, got, ref in zip(owns, gots, outs, strict=True):
            value = products(*parts, own, got)
            for k in range(NA):
                ref[k] = value[k].astype(bf16)

    far = jax.ShapeDtypeStruct((NA, EXITS, HALF), bf16)
    own, other = weights
    return pl.pallas_call(
        kernel,
        out_shape=tuple(jax.ShapeDtypeStruct((EXITS, VDEV), bf16) for _ in range(3)) + (far,) * len(rounds),
        grid_spec=pltpu.PrefetchScalarGridSpec(
            num_scalar_prefetch=1,
            grid=(1,),
            in_specs=[
                whole((1, EXITS)),
                whole((1, EXITS)),
                whole((EXITS, 2 * VDEV)),
                whole((8, EXITS)),
            ]
            + weight_specs(rounds),
            out_specs=tuple(whole((EXITS, VDEV)) for _ in range(3))
            + (whole(far.shape),) * len(rounds),
        ),
        compiler_params=params(),
        cost_estimate=cost(300_000_000, 3_500_000),
        name="logit_gradients",
    )(starts, labels, weight, logits, stats, *[own] * len(rounds), *[other] * len(rounds))


def head_gradient(core, own, got, dl, part, parts, before):
    per = 4
    steps = NV // per // parts
    first = before is None

    def kernel(t, p, q, d, *rest):
        out = rest[-1]
        for ref, side in ((p, t[0]), (q, 1 - t[0])):
            left = jnp.concatenate([ref[k] for k in range(per)], axis=1)
            value = lax.dot_general(
                left, d[...], (((0,), (0,)), ((), ())), preferred_element_type=f32
            ).astype(bf16)
            for k in range(per):
                at = pl.multiple_of(2 * k * HALF + side * HALF, HALF)
                out[pl.ds(at, HALF), :] = value[k * HALF : (k + 1) * HALF]

    block = pl.BlockSpec((per, EXITS, HALF), lambda i, t: (i + part * steps, 0, 0))
    return pl.pallas_call(
        kernel,
        out_shape=jax.ShapeDtypeStruct((D, VDEV), bf16),
        grid_spec=pltpu.PrefetchScalarGridSpec(
            num_scalar_prefetch=1,
            grid=(steps,),
            in_specs=[block, block, whole((EXITS, VDEV))]
            + ([] if first else [pl.BlockSpec(memory_space=pl.ANY)]),
            out_specs=pl.BlockSpec((2 * HALF * per, VDEV), lambda i, t: (i + part * steps, 0)),
        ),
        input_output_aliases={} if first else {4: 0},
        compiler_params=params(MORE_BYTES),
        cost_estimate=cost(2 * EXITS * D * VDEV // parts, 13_000_000 // parts),
        name="head_gradient",
    )(core, own, got, dl, *([] if first else [before]))


def row_tables(mask, targets, section_weight):
    def kernel(mask, targets, weight, table, labels, weights):
        row = lax.broadcasted_iota(jnp.int32, (EXITS, 1), 0).astype(f32)
        upper = lax.broadcasted_iota(jnp.int32, (256, 256), 0) <= lax.broadcasted_iota(
            jnp.int32, (256, 256), 1
        )
        upper = upper.astype(bf16)
        label = jnp.zeros((EXITS, 1), f32)
        scale = jnp.zeros((EXITS, 1), f32)
        base = jnp.int32(0)
        for s in range(NX * NC):
            m = mask[:, s * 256 : (s + 1) * 256]
            number = jnp.sum(m)
            table[s], table[8 + s] = base, number
            live = jnp.broadcast_to(m.astype(f32), (8, 256)).astype(bf16)
            rank = jnp.dot(live, upper, preferred_element_type=f32)[0:1]
            place = jnp.where(m == 1, rank + (base - 1).astype(f32), -1.0)
            goal = targets[:, s * 256 : (s + 1) * 256].astype(f32)
            label += jnp.sum(jnp.where(place == row, goal, 0.0), axis=1, keepdims=True)
            at = row - base.astype(f32)
            scale += jnp.where((at >= 0.0) & (at < number.astype(f32)), weight[s], 0.0)
            base = base + number
        labels[...] = to_row(label)
        weights[...] = to_row(scale)

    vmem, smem = pl.BlockSpec(memory_space=pltpu.VMEM), pl.BlockSpec(memory_space=pltpu.SMEM)
    return pl.pallas_call(
        kernel,
        out_shape=(
            jax.ShapeDtypeStruct((16,), jnp.int32),
            jax.ShapeDtypeStruct((1, EXITS), f32),
            jax.ShapeDtypeStruct((1, EXITS), f32),
        ),
        in_specs=[vmem, vmem, smem],
        out_specs=(smem, vmem, vmem),
        cost_estimate=cost(4_000_000, 500_000),
        name="row_tables",
    )(mask, targets, section_weight)


def sum_blocks(*blocks):
    def kernel(*refs):
        ins, outs = refs[:6], refs[6:]
        for i in range(2):
            own, left, right = ins[3 * i : 3 * i + 3]
            for k in range(NA):
                value = own[k].astype(f32) + (left[k].astype(f32) + right[k].astype(f32))
                outs[i * NA + k][0] = value.astype(bf16)

    return pl.pallas_call(
        kernel,
        out_shape=tuple(jax.ShapeDtypeStruct((1, EXITS, HALF), bf16) for _ in range(NZ)),
        cost_estimate=cost(1_000_000, 3_200_000),
        name="sum_blocks",
    )(*blocks[0], *blocks[1])


def thirds(value):
    hi = value.astype(bf16).astype(f32)
    mid = (value - hi).astype(bf16).astype(f32)
    low = value - hi - mid
    pad = jnp.zeros((16 - 3 * value.shape[0], HALF), f32)
    return jnp.concatenate([hi, mid, low, pad], axis=0).astype(bf16)


def select_rows(mask, gain, hidden):
    def kernel(mask, gain, hidden, hit, rows, keep, give):
        x, c = lax.axis_index("x"), lax.axis_index("core")
        upper = lax.broadcasted_iota(jnp.int32, (256, 256), 0) <= lax.broadcasted_iota(
            jnp.int32, (256, 256), 1
        )
        m = mask[:, pl.ds(pl.multiple_of((x * NC + c) * 256, 256), 256)]
        live = jnp.broadcast_to(m.astype(f32), (8, 256)).astype(bf16)
        rank = jnp.dot(live, upper.astype(bf16), preferred_element_type=f32)[0:1]
        place = jnp.where(m == 1, rank - 1.0, -1.0)
        slot = lax.broadcasted_iota(jnp.int32, (CAP, 1), 0).astype(f32)
        chosen = jnp.where(place == slot, 1.0, 0.0).astype(bf16)
        hit[...] = chosen
        value = jnp.dot(chosen, hidden[...], preferred_element_type=f32).astype(bf16)
        rows[...] = value
        first = c == 0
        left, right = value[:, :HALF], value[:, HALF:]
        keep[:CAP, :] = jnp.where(first, left, right)
        give[...] = jnp.where(first, right, left)
        keep[CAP:, :] = thirds(jnp.where(first, gain[0:1], gain[1:2]))

    return pl.pallas_call(
        kernel,
        out_shape=(
            jax.ShapeDtypeStruct((CAP, 256), bf16),
            jax.ShapeDtypeStruct((CAP, 256), bf16),
            jax.ShapeDtypeStruct((CAP + 16, HALF), bf16),
            jax.ShapeDtypeStruct((CAP, HALF), bf16),
        ),
        cost_estimate=cost(20_000_000, 300_000),
        name="select_rows",
    )(mask, gain, hidden)


def compact_rows(table, pairs_of):
    def kernel(t, p0, p1, p2, p3, rows, slab):
        at = lax.broadcasted_iota(jnp.int32, (EXITS, CAP), 0)
        slot = lax.broadcasted_iota(jnp.int32, (EXITS, CAP), 1)
        x, c = lax.axis_index("x"), lax.axis_index("core")
        total = jnp.zeros((EXITS, HALF), f32)
        for k, ref in enumerate((p0, p1, p2, p3)):
            for j in range(NC):
                s = lax.rem(x + k, NX) * NC + (c if j == 0 else 1 - c)
                hit = (at - slot == t[s]) & (slot < t[8 + s])
                hit = jnp.where(hit, 1.0, 0.0).astype(bf16)
                first = j * (CAP + 16)
                total += jnp.dot(hit, ref[first : first + CAP, :], preferred_element_type=f32)
        rows[...] = total.astype(bf16)
        scale = p0[CAP : CAP + 16, :].astype(f32)
        scale = scale[0:1] + scale[1:2] + scale[2:3]
        slab[0, :EXITS, :] = (total * scale).astype(bf16)
        sq = to_row(jnp.sum(total * total, axis=1, keepdims=True))
        sq = jnp.concatenate([sq[:, k : k + HALF] for k in range(0, EXITS, HALF)], axis=0)
        slab[0, EXITS:, :] = thirds(sq)

    return pl.pallas_call(
        kernel,
        out_shape=(
            jax.ShapeDtypeStruct((EXITS, HALF), bf16),
            jax.ShapeDtypeStruct((1, ROWS, HALF), bf16),
        ),
        grid_spec=pltpu.PrefetchScalarGridSpec(
            num_scalar_prefetch=1,
            grid=(1,),
            in_specs=[whole((PACK, HALF))] * NX,
            out_specs=(whole((EXITS, HALF)), whole((1, ROWS, HALF))),
        ),
        compiler_params=params(MORE_BYTES),
        cost_estimate=cost(80_000_000, 500_000),
        name="compact_rows",
    )(table, *pairs_of)


def spread_rows(table, inverse, rows, parts):
    def kernel(t, inverse, rows, *refs):
        outs = refs[NZ:]
        grads = tree([ref[0].astype(f32) for ref in refs[:NZ]])
        inv = to_column(inverse[...])
        gain = jnp.sum(grads * rows[...].astype(f32) * inv, axis=0, keepdims=True)
        tail = thirds(gain)
        slot = lax.broadcasted_iota(jnp.int32, (CAP, EXITS), 0)
        at = lax.broadcasted_iota(jnp.int32, (CAP, EXITS), 1)
        x, c = lax.axis_index("x"), lax.axis_index("core")
        value = grads.astype(bf16)
        for k, ref in enumerate(outs):
            for j in range(NC):
                s = lax.rem(x + k, NX) * NC + (c if j == 0 else 1 - c)
                hit = (at - slot == t[s]) & (slot < t[8 + s])
                hit = jnp.where(hit, 1.0, 0.0).astype(bf16)
                ref[j * CAP : (j + 1) * CAP, :] = jnp.dot(
                    hit, value, preferred_element_type=f32
                ).astype(bf16)
            ref[NC * CAP :, :] = tail

    shape = (PACK, HALF)
    return pl.pallas_call(
        kernel,
        out_shape=tuple(jax.ShapeDtypeStruct(shape, bf16) for _ in range(NX)),
        grid_spec=pltpu.PrefetchScalarGridSpec(
            num_scalar_prefetch=1,
            grid=(1,),
            in_specs=[whole((1, EXITS)), whole((EXITS, HALF))] + [whole((1, EXITS, HALF))] * NZ,
            out_specs=tuple(whole(shape) for _ in range(NX)),
        ),
        compiler_params=params(MORE_BYTES),
        cost_estimate=cost(80_000_000, 700_000),
        name="spread_rows",
    )(table, inverse, rows, *parts)


def finish(table, stats, weight, gain, keep, came, rows, hit):
    def kernel(t, stats, w, gain, keep, came, rows, hit, hidden, out):
        x, c = lax.axis_index("x"), lax.axis_index("core")
        top, total, moment, picked, inverse = (stats[k : k + 1] for k in range(5))
        inner = w[...] * ((top - picked) + moment / total) / (inverse * D)
        at = lax.broadcasted_iota(jnp.int32, (CAP, EXITS), 1)
        slot = lax.broadcasted_iota(jnp.int32, (CAP, EXITS), 0)
        mine = at - slot == t[x * NC + c]
        inverse, inner = (
            jnp.sum(jnp.where(mine, q, 0.0), axis=1, keepdims=True) for q in (inverse, inner)
        )
        first = c == 0
        left = jnp.where(first, keep[...], came[...])
        right = jnp.where(first, came[...], keep[...])
        grads = jnp.concatenate([left[:CAP], right[:CAP]], axis=1)
        scale = jnp.concatenate([gain[0:1], gain[1:2]], axis=1)
        value = inverse * (grads * scale) - rows[...].astype(f32) * (
            inverse * inverse * inverse * inner
        )
        hidden[...] = lax.dot_general(
            hit[...], value.astype(bf16), (((0,), (0,)), ((), ())), preferred_element_type=f32
        ).astype(bf16)
        out[...] = jnp.concatenate([left[CAP : CAP + 1], right[CAP : CAP + 1]], axis=1)

    return pl.pallas_call(
        kernel,
        out_shape=(
            jax.ShapeDtypeStruct((256, 2 * HALF), bf16),
            jax.ShapeDtypeStruct((1, 2 * HALF), f32),
        ),
        grid_spec=pltpu.PrefetchScalarGridSpec(
            num_scalar_prefetch=1,
            grid=(1,),
            in_specs=[
                whole((8, EXITS)),
                whole((1, EXITS)),
                whole((NC, HALF)),
                whole((CAP + 8, HALF)),
                whole((CAP + 8, HALF)),
                whole((CAP, 2 * HALF)),
                whole((CAP, 256)),
            ],
            out_specs=(whole((256, 2 * HALF)), whole((1, 2 * HALF))),
        ),
        compiler_params=params(),
        cost_estimate=cost(13_000_000, 500_000),
        name="finish",
    )(table, stats, weight, gain, keep, came, rows, hit)


def together(*values):
    return lax.optimization_barrier(values)


def after(value, *others):
    return lax.optimization_barrier((value, *others))[0]


def body(hidden, norm_gain, head_weight, exit_mask, targets, section_weight):
    x, c = lax.axis_index("x").astype(jnp.int32), lax.axis_index("core").astype(jnp.int32)
    y, z = lax.axis_index("y"), lax.axis_index("z")
    section = x * NC + c

    mask = exit_mask.reshape(1, -1)
    own_hit, rows_own, keep, give = select_rows(mask, norm_gain.reshape(NC, HALF), hidden)
    pack = jnp.concatenate([keep, swap(give)], axis=0)
    row_table, labels, row_weight = row_tables(
        after(mask, pack), targets.reshape(1, -1), section_weight
    )
    rows, slab = compact_rows(row_table, [fetch(pack, k) for k in range(NX)])

    table = lax.dynamic_slice(jnp.asarray(TABLE), (c, x, y, z, 0), (1, 1, 1, 1, 2 * NV + 3))
    table = table.reshape(-1)

    give = split_weights(after(table, slab), head_weight, 1)
    came = [shift(slab, "z", -k) for k in STEPS[1:]]
    *came, give = together(*came, give)
    own_weights = split_weights(after(table, give), head_weight, 0)
    near_a = jnp.concatenate([slab, *came[: NA - 1]], axis=0)
    near_b = jnp.concatenate(came[NA - 1 :], axis=0)
    left_a, right_b = send(near_a, 1), send(near_b, -1)
    left_b, right_a = send(near_b, 1), send(near_a, -1)
    weights = own_weights, swap(give)
    far_a, far_b = send(left_a, 1), send(right_b, -1)
    add = functools.partial(add_logits, table, weights)
    part = add([0, 1], [near_a, near_b], None)
    left_b, right_a = after(left_b, part[0]), after(right_a, part[0])
    part = add([2, 6, 3, 7], [right_a, left_a, right_b, left_b], part)
    far_a, far_b = after(far_a, part[0]), after(far_b, part[0])
    part, acts = add([4, 5], [far_a, far_b], part)

    logits, stats = softmax_parts(table, labels, part, swap(part))
    other_acts = swap(after(acts, stats))
    for axis in ("x", "y", "z"):
        stats = merge(stats, axis)
    top, total, _, picked, inverse = (stats[k] for k in range(5))
    mean_loss = jnp.sum(top + jnp.log(total) - picked) / EXITS
    dl_own, dl_got, dl_scaled, far_a, far_b, right_b, left_a = logit_gradients(
        table, labels, row_weight, logits, stats, weights, [4, 5, 3, 6]
    )

    grad = functools.partial(gradient_blocks, table, weights, dl_own, dl_got)
    head = functools.partial(head_gradient, c[None], acts, other_acts)
    parts = 4
    come_a, come_b = send(far_a, 1), send(far_b, -1)
    from_left_b, from_right_a = send(right_b, 1), send(left_a, -1)
    right_a, left_b, own_a, own_b = grad([2, 7, 0, 1])
    come_a, come_b, from_left_b, from_right_a, right_a, left_b = together(
        come_a, come_b, from_left_b, from_right_a, right_a, left_b
    )
    right_a, left_b = right_a + come_a, left_b + come_b
    from_left_a, from_right_b = send(right_a, 1), send(left_b, -1)
    d_head = head(after(dl_scaled, right_a, left_b), 0, parts, None)
    from_left_a, from_right_b, d_head = together(from_left_a, from_right_b, d_head)

    sums = sum_blocks((own_a, from_left_a, from_right_a), (own_b, from_left_b, from_right_b))
    came = [shift(q, "z", k) for q, k in zip(sums[1:], STEPS[1:], strict=True)]
    d_head = head(after(dl_scaled, sums[0]), 1, parts, d_head)
    d_head = head(dl_scaled, 2, parts, d_head)
    *came, d_head = together(*came, d_head)
    packs = spread_rows(row_table, inverse[None], rows, [sums[0]] + came)
    came = [deliver(packs[k], k) for k in range(NX)]
    d_head = head(after(dl_scaled, packs[0]), 3, parts, d_head)
    *came, d_head = together(*came, d_head)
    joined = tree([p.astype(f32) for p in came])
    gain_sum = joined[NC * CAP] + joined[NC * CAP + 1] + joined[NC * CAP + 2]
    keep, give = joined[:CAP], joined[CAP : NC * CAP]
    keep = jnp.concatenate([keep, jnp.broadcast_to(gain_sum[None], (8, HALF))], axis=0)
    give = jnp.concatenate([give, jnp.broadcast_to(gain_sum[None], (8, HALF))], axis=0)
    d_hidden, d_gain = finish(
        row_table, stats, row_weight, norm_gain.reshape(NC, HALF), keep, swap(give), rows_own, own_hit
    )
    d_gain = d_gain.reshape(-1)
    return (mean_loss, d_hidden, d_gain, d_head)


def solution(mesh):
    fine = Mesh(mesh.devices.reshape(NX, NC, NY, NZ), AXES)
    s, v = ("x", "core"), ("y", "z")
    return jax.shard_map(
        body,
        mesh=fine,
        in_specs=(P(s, v), P(v), P(None, AXES), P(), P(), P()),
        out_specs=(P(), P(s, v), P(v), P(None, AXES)),
        check_vma=False,
    )
```
